256 devices in a mesh: pipe: 8 (over y, core), tensor: 16 (over x, z_hi), dp: 2 (over z_lo).
Axes of the slice: x: 4, y: 4, z: 8 (z_hi: 4, z_lo: 2; z = z_hi * 2 + z_lo), core: 2. Of those that a mesh axis runs over, the one named last changes fastest.
Arguments:
- hidden: bfloat16 [8, 2, 512, 8192], P('pipe', None, 'dp', 'tensor'), may hold values from -6 to 6
- query_weight: bfloat16 [8, 2, 8192, 4096], P('pipe', None, 'dp', 'tensor'), as said below
- keyval_weight: bfloat16 [8, 2, 8192, 1024], P('pipe', None, 'dp', 'tensor'), as said below
- doc_ids: int32 [8, 2, 2, 256], P('pipe', None, 'dp'), may hold values from 0 to 3, never falling along the last dimension, each value on 1 to 128 neighbouring positions
- cotangent: bfloat16 [8, 2, 512, 4096], P('pipe', None, 'dp', 'tensor'), may hold values from -6 to 6
Outputs:
- attended: bfloat16 [8, 2, 512, 4096], P('pipe', None, 'dp', 'tensor')
- hidden_grad: bfloat16 [8, 2, 512, 8192], P('pipe', None, 'dp', 'tensor')
- query_grad: float32 [8, 8192, 4096], P('pipe', 'dp', 'tensor')
- slab_keyvalue_gradient: float32 [8, 8192, 1024], P('pipe', 'dp', 'tensor')
The draws below stay inside these ranges and needn't reach their ends.
Inputs may be any that keep to these rules, and one draw needn't show every extreme that they name: `doc_ids`: along the last dimension ids never fall; each document holds 1 to 128 tokens, one exactly 128. query_weight[p, 1] equals query_weight[7 - p, 0] for every p. keyval_weight[p, 1] equals keyval_weight[7 - p, 0] for every p.
All inputs are finite; a program needn't handle non-finite values.
Results may differ from the reference program's by a relative error of at most 0.025.
Values may be sent and summed in bfloat16 or wider, within the bound.
A program may use at most 128 MiB of HBM per device.

```python
import math
import jax
import jax.numpy as jnp
import numpy as np

MODEL_WIDTH = 8192
QUERY_HEADS = 32
KEYVALUE_HEADS = 4
HEAD_SIZE = 128
MB = 256
DOCS = 4
ROWS = 512
N_PIPE = 8
N_DP = 2


def local_weight_pair(key, columns, spread):
    base = jnp.clip(jax.random.normal(key, (N_PIPE, MODEL_WIDTH, columns), jnp.float32), -6.0, 6.0)
    base = base * spread
    return jnp.stack([base, base[::-1]], axis=1).astype(jnp.bfloat16)


def draw_query_weight(key, part):
    key = jax.random.fold_in(key, 11)
    return local_weight_pair(key, QUERY_HEADS * HEAD_SIZE, MODEL_WIDTH ** (-0.5))


def draw_keyval_weight(key, part):
    key = jax.random.fold_in(key, 23)
    return local_weight_pair(key, 2 * KEYVALUE_HEADS * HEAD_SIZE, MODEL_WIDTH ** (-0.5))


def with_spikes(entries, key, source, target, parts, factor):
    owner, partner = [(jnp.arange(entries.shape[axis_at]) // (entries.shape[axis_at] // parts)).reshape([-1 if axis == axis_at else 1 for axis in range(entries.ndim)]) for axis_at in (source, target)]
    chosen = jax.random.permutation(key, parts)[partner]
    strong = (owner == chosen) | (owner == (partner + parts // 2) % parts)
    return jnp.where(strong, factor * entries, entries)


def levels(rng, extent, pieces, low, top_value):
    factor_of = 1.0
    for axis_at, parts in pieces:
        draws = jax.random.uniform(jax.random.fold_in(jax.random.fold_in(rng, 6), axis_at), (parts,), jnp.float32, low / len(pieces), top_value / len(pieces))
        factor_of = factor_of * jnp.repeat(jnp.exp(draws), extent[axis_at] // parts).reshape((-1,) + (1,) * (len(extent) - 1 - axis_at))
    return factor_of


def length_profile(number_of, total, bound, lean):
    portions = [(1 << 20) // math.isqrt(grade ** lean) + 1 for grade in range(2, number_of + 1)]
    surplus, holding = total - bound - (number_of - 1), [1] * (number_of - 1)
    while surplus > 0:
        candidates = [i for i in range(number_of - 1) if holding[i] < bound]
        whole, left = sum([portions[i] for i in candidates]), surplus
        for i in candidates:
            extra = min(bound - holding[i], max(1, left * portions[i] // whole), surplus)
            holding[i] = holding[i] + extra
            surplus = surplus - extra
    return np.array([bound] + holding)


def uneven_parts(own_key, count, total, most, lean):
    if count == 2:
        one = jax.random.randint(own_key, (), max(1, total - most), min(most, total - 1) + 1)
        return jnp.stack([one, total - one])
    tallies = jnp.asarray(length_profile(count, total, most, lean), jnp.int32)
    pairs = (count - 1) // 2
    giver, taker = tallies[1:1 + 2 * pairs:2], tallies[2:2 + 2 * pairs:2]
    slack = jnp.minimum(giver - 1, most - taker)
    passed = jax.random.randint(jax.random.fold_in(own_key, 1), (pairs,), 0, 1 << 20) % (slack + 1)
    tallies = tallies.at[1:1 + 2 * pairs:2].set(giver - passed).at[2:2 + 2 * pairs:2].set(taker + passed)
    return tallies[jax.random.permutation(jax.random.fold_in(own_key, 2), count)]


def scatter_about(rng, dims, width, most, pieces=(), held_as=jnp.bfloat16):
    entries = width * jax.random.normal(rng, dims, jnp.float32)
    if pieces:
        entries = entries * levels(rng, dims, pieces, -0.22, 0.18)
    return jnp.clip(entries, -most, most).astype(held_as)


def gaussian_with(rng, extent, scale, bound, pieces, heavy, kind=jnp.bfloat16):
    array = scale * jax.random.normal(rng, extent, jnp.float32)
    if pieces:
        array = array * levels(rng, extent, pieces, -0.22, 0.18)
    return jnp.clip(with_spikes(array, jax.random.fold_in(rng, 3), *heavy), -bound, bound).astype(kind)


def setup_inputs(seed: int = 0) -> dict:
    seeds = jax.random.split(jax.random.key(seed), 6)
    return {
        "hidden": scatter_about(seeds[0], (N_PIPE, 2, ROWS, MODEL_WIDTH), 1.0, 6.0, ((0, 8), (2, 2), (3, 16))),
        "query_weight": draw_query_weight(jax.random.fold_in(seeds[5], 71), 0),
        "keyval_weight": draw_keyval_weight(jax.random.fold_in(seeds[5], 71), 0),
        "doc_ids": jax.vmap(lambda own: jnp.searchsorted(jnp.cumsum(uneven_parts(own, DOCS, MB, MB // 2, 0)), jnp.arange(MB), side="right"))(jax.random.split(seeds[3], N_PIPE * 2 * N_DP)).reshape((N_PIPE, 2, N_DP, MB)).astype(jnp.int32),
        "cotangent": gaussian_with(seeds[4], (N_PIPE, 2, ROWS, QUERY_HEADS * HEAD_SIZE), 1.0, 6.0, ((0, 8), (2, 2), (3, 16)), (3, 2, 16, 2.0)),
    }


def tables(sequence_length):
    positions = jnp.arange(sequence_length, dtype=jnp.float32)
    freqs = 10000.0 ** (-2.0 * jnp.arange(HEAD_SIZE // 2, dtype=jnp.float32) / HEAD_SIZE)
    angles = positions[:, None] * freqs[None, :]
    return jnp.cos(angles), jnp.sin(angles)


def rotate(values, cosine_table, sine_table):
    half_width = values.shape[-1] // 2
    first, second = values[..., :half_width], values[..., half_width:]
    return jnp.concatenate([first * cosine_table - second * sine_table, second * cosine_table + first * sine_table], -1)


def inverse_rotation(values, cosine_table, sine_table):
    half_width = values.shape[-1] // 2
    first, second = values[..., :half_width], values[..., half_width:]
    return jnp.concatenate([first * cosine_table + second * sine_table, second * cosine_table - first * sine_table], -1)


def one_piece(input_rows, query_slab, keyvalue_piece, doc_row, grad_in):
    sequence_length = input_rows.shape[0]
    cosine_table, sine_table = tables(sequence_length)
    cosine_broadcast, sine_broadcast = cosine_table[:, None], sine_table[:, None]
    head_ratio = QUERY_HEADS // KEYVALUE_HEADS
    score_scale = HEAD_SIZE ** -0.5
    queries = jnp.dot(input_rows, query_slab, preferred_element_type=jnp.float32).reshape(sequence_length, QUERY_HEADS, HEAD_SIZE)
    queries = rotate(queries, cosine_broadcast, sine_broadcast).astype(jnp.bfloat16)
    projected_rows = jnp.dot(input_rows, keyvalue_piece, preferred_element_type=jnp.float32).reshape(sequence_length, KEYVALUE_HEADS, 2, HEAD_SIZE)
    keys = rotate(projected_rows[:, :, 0], cosine_broadcast, sine_broadcast).astype(jnp.bfloat16)
    values = projected_rows[:, :, 1].astype(jnp.bfloat16)
    keys_wide = jnp.repeat(keys, head_ratio, axis=1).astype(jnp.float32)
    values_wide = jnp.repeat(values, head_ratio, axis=1).astype(jnp.float32)
    queries_f = queries.astype(jnp.float32)
    scores = jnp.einsum('qhd,khd->hqk', queries_f, keys_wide) * score_scale
    token_index = jnp.arange(sequence_length)
    allowed = (token_index[None, :] <= token_index[:, None]) & (doc_row[:, None] == doc_row[None, :])
    weights = jnp.where(allowed[None], jnp.exp(scores), 0.0)
    probs_full = weights / jnp.sum(weights, axis=-1, keepdims=True)
    probs_low = probs_full.astype(jnp.bfloat16).astype(jnp.float32)
    attended = jnp.einsum('hqk,khd->qhd', probs_low, values_wide).astype(jnp.bfloat16)
    grad_out = grad_in.reshape(sequence_length, QUERY_HEADS, HEAD_SIZE).astype(jnp.float32)
    value_gradient = jnp.einsum('hqk,qhd->khd', probs_low, grad_out)
    grad_probs = jnp.einsum('qhd,khd->hqk', grad_out, values_wide)
    row_dot = jnp.sum(grad_probs * probs_full, axis=-1, keepdims=True)
    grad_scores = (probs_full * (grad_probs - row_dot) * score_scale).astype(jnp.bfloat16).astype(jnp.float32)
    query_gradient = jnp.einsum('hqk,khd->qhd', grad_scores, keys_wide)
    query_gradient = inverse_rotation(query_gradient, cosine_broadcast, sine_broadcast).astype(jnp.bfloat16).reshape(sequence_length, QUERY_HEADS * HEAD_SIZE)
    key_gradient = jnp.einsum('hqk,qhd->khd', grad_scores, queries_f)
    key_gradient = inverse_rotation(key_gradient, cosine_broadcast, sine_broadcast).reshape(sequence_length, KEYVALUE_HEADS, head_ratio, HEAD_SIZE).sum(2)
    value_gradient = value_gradient.reshape(sequence_length, KEYVALUE_HEADS, head_ratio, HEAD_SIZE).sum(2)
    keyvalue_gradient = jnp.stack([key_gradient, value_gradient], axis=2).astype(jnp.bfloat16).reshape(sequence_length, KEYVALUE_HEADS * 2 * HEAD_SIZE)
    hidden_part = jnp.dot(query_gradient, query_slab.T, preferred_element_type=jnp.float32)
    hidden_part = (hidden_part + jnp.dot(keyvalue_gradient, keyvalue_piece.T, preferred_element_type=jnp.float32)).astype(jnp.bfloat16)
    query_part = jnp.dot(input_rows.T, query_gradient, preferred_element_type=jnp.float32).astype(jnp.bfloat16)
    keyval_part = jnp.dot(input_rows.T, keyvalue_gradient, preferred_element_type=jnp.float32).astype(jnp.bfloat16)
    return attended.reshape(sequence_length, QUERY_HEADS * HEAD_SIZE), hidden_part, query_part, keyval_part


def reference(hidden, query_weight, keyval_weight, doc_ids, cotangent):
    query_grad = jnp.zeros((N_PIPE, MODEL_WIDTH, QUERY_HEADS * HEAD_SIZE), jnp.float32)
    slab_keyvalue_gradient = jnp.zeros((N_PIPE, MODEL_WIDTH, 2 * KEYVALUE_HEADS * HEAD_SIZE), jnp.float32)
    attended_all = []
    hidden_all = []
    for position in range(N_PIPE):
        attended_dirs = []
        hidden_dirs = []
        for direction in range(2):
            slab_index = position if direction == 0 else N_PIPE - 1 - position
            attended_rows = []
            hidden_rows = []
            for replica in range(N_DP):
                row_start = replica * MB
                input_rows = hidden[position, direction, row_start:row_start + MB]
                grad_in = cotangent[position, direction, row_start:row_start + MB]
                attended, hidden_part, query_part, keyval_part = one_piece(
                    input_rows, query_weight[position, direction], keyval_weight[position, direction],
                    doc_ids[position, direction, replica], grad_in)
                attended_rows.append(attended)
                hidden_rows.append(hidden_part)
                query_grad = query_grad.at[slab_index].add(query_part.astype(jnp.float32))
                slab_keyvalue_gradient = slab_keyvalue_gradient.at[slab_index].add(keyval_part.astype(jnp.float32))
            attended_dirs.append(jnp.concatenate(attended_rows, 0))
            hidden_dirs.append(jnp.concatenate(hidden_rows, 0))
        attended_all.append(jnp.stack(attended_dirs))
        hidden_all.append(jnp.stack(hidden_dirs))
    return jnp.stack(attended_all), jnp.stack(hidden_all), query_grad, slab_keyvalue_gradient
```

```python
import jax
import jax.numpy as jnp
import numpy as np
from jax import lax
from jax.experimental import pallas as pl
from jax.experimental.pallas import tpu as pltpu
from jax.sharding import PartitionSpec as P

MESH = pl.DeviceIdType.MESH
HEAD = 128
TOK = 256
FEAT = 512
F32 = jnp.float32
BF16 = jnp.bfloat16
FLOWS = ((0, 256, "z"),)


def dot(a, b, ca, cb):
    return lax.dot_general(a, b, (((ca,), (cb,)), ((), ())), preferred_element_type=F32)


def pack(v):
    return jnp.concatenate([v[: TOK // 2], v[TOK // 2 :]], axis=1)


def unpack(v):
    v = v.astype(F32)
    return jnp.concatenate([v[:, :64], v[:, 64:]], axis=0)


def kernel(
    hid, wq, wkv, doc, cot, cosf, sinf,
    att_out, hg_out, gq_out, gkv_out,
    X, Wq, Wkv, C, docs, Pq, Pkv, sPq, sPkv, rPq, rPkv, KV, gfp, gsb, grb, Gq, Gkvp, Gkv, Qb, Kb, Vb, att,
    sd, sp, sm, rd, rp, rm, zsd, zsp, zsm, zrd, zrp, zrm, fin, wgq, wgkv,
    ss, rr, ra, ls,
):
    pipe, tens, zl = lax.axis_index("pipe"), lax.axis_index("tensor"), lax.axis_index("dp")
    x, zh = lax.div(tens, 4), lax.rem(tens, 4)
    y, c = lax.div(pipe, 2), lax.rem(pipe, 2)
    own = lax.div(x, 2) == zl

    def dev(x, y, zh, zl, c):
        return {"pipe": y * 2 + c, "tensor": x * 4 + zh, "dp": zl}

    def up(v, k):
        return lax.rem(v + k + 4, 4)

    zflip = 1 - zl
    neighbour = {
        ("x", 1): dev(up(x, 1), y, zh, zl, c),
        ("x", -1): dev(up(x, -1), y, zh, zl, c),
        ("z", 1): dev(x, y, up(zh, 1), zl, c),
        ("z", -1): dev(x, y, up(zh, -1), zl, c),
        ("z", 2): dev(x, y, up(zh, 2), zl, c),
    }
    partner = dev(x, y, zh, zflip, c)
    mirror = dev(x, 3 - y, zh, zl, 1 - c)
    swap0 = dev(3 - x, y, zh, zflip, c)
    swap1 = dev(jnp.where(own, x, 3 - x), 3 - y, zh, jnp.where(own, zl, zflip), 1 - c)

    count = {"s": 0, "r": 0, "l": 0}
    pending = []

    def take(kind):
        count[kind] += 1
        return count[kind] - 1

    def send(src, dst, rsem, to):
        copy = pltpu.make_async_remote_copy(
            src_ref=src, dst_ref=dst, send_sem=ss.at[take("s")], recv_sem=rsem, device_id=to, device_id_type=MESH
        )
        copy.start()
        pending.append(copy)

    def arrived(dst, rsem, frm):
        pltpu.make_async_remote_copy(
            src_ref=dst, dst_ref=dst, send_sem=ss.at[0], recv_sem=rsem, device_id=frm, device_id_type=MESH
        ).wait_recv()

    def local(src, dst):
        copy = pltpu.make_async_copy(src, dst, ls.at[take("l")])
        copy.start()
        return copy

    load_wq = local(wq.at[0], Wq)
    load_wkv = local(wkv.at[0], Wkv)
    load_c = local(cot.at[0], C.at[0])

    barrier = pltpu.get_barrier_semaphore()
    greet0 = dev(
        jnp.where(own, x, 3 - x), jnp.where(own, 3 - y, y), zh, jnp.where(own, zl, zflip), jnp.where(own, 1 - c, c)
    )
    for to in list(neighbour.values()) + [partner, mirror, swap1, greet0]:
        pl.semaphore_signal(barrier, inc=1, device_id=to, device_id_type=MESH)
    pl.semaphore_wait(barrier, 9)

    s1r = rr.at[take("r")]
    send(hid.at[1], X.at[1, jnp.where(own, x, 3 - x), zh], s1r, swap1)
    s0s, s0r, s0l = ss.at[take("s")], rr.at[take("r")], ls.at[take("l")]

    @pl.when(own)
    def _():
        copy = pltpu.make_async_copy(hid.at[0], X.at[0, x, zh], s0l)
        copy.start()
        copy.wait()

    @pl.when(jnp.logical_not(own))
    def _():
        copy = pltpu.make_async_remote_copy(
            src_ref=hid.at[0], dst_ref=X.at[0, 3 - x, zh], send_sem=s0s, recv_sem=s0r, device_id=swap0, device_id_type=MESH
        )
        copy.start()
        copy.wait()

    Pq[...] = jnp.zeros_like(Pq)
    Pkv[...] = jnp.zeros_like(Pkv)

    cr, dr = rr.at[take("r")], rr.at[take("r")]

    def send_small():
        send(cot.at[1], C.at[1], cr, mirror)
        send(doc.at[1], docs, dr, mirror)

    def block(xs, zs):
        bit = lax.rem(lax.rem(xs, 2) + lax.div(xs, 2) + zl, 2)
        return pl.multiple_of((bit * 4 + zs) * FEAT, FEAT)

    def project(e, xs, zs):
        d = lax.div(xs, 2)
        rows = pl.ds(block(xs, zs), FEAT)
        xb = X[e, xs, zs]
        Pq[e, d] += dot(xb, Wq[rows, :], 1, 0)
        Pkv[e, d] += dot(xb, Wkv[rows, :], 1, 0)

    pos = {"x": x, "z": zh}

    def slot(first, a, b):
        return (a, b) if first == "x" else (b, a)

    def part(flow, half):
        r0, n, _ = FLOWS[flow]
        if half is None:
            return pl.ds(r0, n)
        return pl.ds(r0 + half * (n // 2), n // 2)

    def fwd(f, e, s, half, axis, sign):
        ref = X.at[e, s[0], s[1], part(f, half)]
        send(ref, ref, ra.at[f, e, s[0], s[1], half or 0], neighbour[(axis, sign)])

    def got(f, e, s, half, axis, sign):
        ref = X.at[e, s[0], s[1], part(f, half)]
        arrived(ref, ra.at[f, e, s[0], s[1], half or 0], neighbour[(axis, sign)])

    def axes(f):
        first = FLOWS[f][2]
        second = "z" if first == "x" else "x"
        return first, second, pos[first], pos[second]

    flows = range(len(FLOWS))

    def gather_first(e):
        for f in flows:
            A, B, a, b = axes(f)
            s = slot(A, a, b)
            fwd(f, e, s, None, A, 1)
            fwd(f, e, s, None, A, -1)
            fwd(f, e, s, None, B, 1)
            fwd(f, e, s, None, B, -1)

    def gather_second(e):
        for f in flows:
            A, B, a, b = axes(f)
            s = slot(A, up(a, -1), b)
            got(f, e, s, None, A, -1)
            fwd(f, e, s, 0, A, 1)
            fwd(f, e, s, None, B, 1)
            fwd(f, e, s, None, B, -1)
            s = slot(A, up(a, 1), b)
            got(f, e, s, None, A, 1)
            fwd(f, e, s, 1, A, -1)
            fwd(f, e, s, None, B, 1)
            fwd(f, e, s, None, B, -1)

    def gather_third(e):
        for f in flows:
            A, B, a, b = axes(f)
            s = slot(A, up(a, 2), b)
            got(f, e, s, 0, A, -1)
            got(f, e, s, 1, A, 1)
            fwd(f, e, s, None, B, 1)
            fwd(f, e, s, None, B, -1)

    def gather_near(e, k):
        for f in flows:
            A, B, a, b = axes(f)
            s = slot(A, up(a, k), up(b, -1))
            got(f, e, s, None, B, -1)
            fwd(f, e, s, 0, B, 1)
            s = slot(A, up(a, k), up(b, 1))
            got(f, e, s, None, B, 1)
            fwd(f, e, s, 1, B, -1)

    def gather_far(e, k):
        for f in flows:
            A, B, a, b = axes(f)
            s = slot(A, up(a, k), up(b, 2))
            got(f, e, s, 0, B, -1)
            got(f, e, s, 1, B, 1)

    ORDER = (0, -1, 1, 2)

    gather_first(0)
    arrived(X.at[1, x, zh], s1r, swap1)
    gather_first(1)
    send_small()
    load_wq.wait()
    load_wkv.wait()
    for e in (0, 1):
        project(e, x, zh)
    for e in (0, 1):
        gather_second(e)
    for e in (0, 1):
        if len(FLOWS) == 1:
            project(e, x, up(zh, -1))
            project(e, x, up(zh, 1))
    for e in (0, 1):
        gather_third(e)
    for e in (0, 1):
        if len(FLOWS) == 1:
            project(e, x, up(zh, 2))
    for k in ORDER:
        for e in (0, 1):
            gather_near(e, k)
            if len(FLOWS) == 1:
                project(e, up(x, -1), up(zh, k))
                project(e, up(x, 1), up(zh, k))
    for k in ORDER:
        for e in (0, 1):
            gather_far(e, k)
            if len(FLOWS) == 1:
                project(e, up(x, 2), up(zh, k))
    if len(FLOWS) > 1:
        for e in (0, 1):
            for i in ORDER:
                for k in ORDER:
                    if (i, k) != (0, 0):
                        project(e, up(x, i), up(zh, k))

    pr = [(rr.at[take("r")], rr.at[take("r")]) for e in (0, 1)]
    for e in (0, 1):
        sPq[e] = Pq[e, zflip].astype(BF16)
        send(sPq.at[e], rPq.at[e], pr[e][0], partner)
        sPkv[e] = pack(Pkv[e, zflip]).astype(BF16)
        send(sPkv.at[e], rPkv.at[e], pr[e][1], partner)

    kvr = [[rr.at[take("r")] for o in (1, 2, 3)] for e in (0, 1)]
    zto = {1: neighbour[("z", 1)], 2: neighbour[("z", 2)], 3: neighbour[("z", -1)]}
    zfrom = {1: neighbour[("z", -1)], 2: neighbour[("z", 2)], 3: neighbour[("z", 1)]}
    for e in (0, 1):
        arrived(rPkv.at[e], pr[e][1], partner)
        piece = pack(Pkv[e, zl]) + rPkv[e].astype(F32)
        KV[e, zh] = piece.astype(BF16)
        for o in (1, 2, 3):
            send(KV.at[e, zh], KV.at[e, zh], kvr[e][o - 1], zto[o])

    cosw, sinw = cosf[...], sinf[...]

    def rope(v):
        return v * cosw + pltpu.roll(v, 64, 1) * sinw

    def unrope(v):
        return v * cosw - pltpu.roll(v, 64, 1) * sinw

    for e in (0, 1):
        arrived(rPq.at[e], pr[e][0], partner)
        q = Pq[e, zl] + rPq[e].astype(F32)
        Qb[e, 0] = rope(q[:, :HEAD]).astype(BF16)
        Qb[e, 1] = rope(q[:, HEAD:]).astype(BF16)

    load_c.wait()
    arrived(C.at[1], cr, mirror)
    arrived(docs, dr, mirror)
    scale = HEAD**-0.5
    ar = [rr.at[take("r")] for _ in (0,)]
    gr = [[rr.at[take("r")] for o in (1, 2, 3)] for e in (0, 1)]
    row = lax.broadcasted_iota(jnp.int32, (TOK, TOK), 0)
    col = lax.broadcasted_iota(jnp.int32, (TOK, TOK), 1)
    for e in (0, 1):
        for o in (1, 2, 3):
            frm = up(zh, -o)
            arrived(KV.at[e, frm], kvr[e][o - 1], zfrom[o])
        kraw = jnp.concatenate([unpack(KV[e, 0]), unpack(KV[e, 1])], axis=1)
        keys = rope(kraw).astype(BF16)
        values = jnp.concatenate([unpack(KV[e, 2]), unpack(KV[e, 3])], axis=1).astype(BF16)
        ids = doc[0] if e == 0 else docs[...]
        wide = jnp.broadcast_to(ids.astype(F32), (TOK, TOK))
        allowed = (wide == wide.T) & (col <= row)
        gk = jnp.zeros((TOK, HEAD), F32)
        gv = jnp.zeros((TOK, HEAD), F32)
        for j in (0, 1):
            q = Qb[e, j]
            g = C[e, :, j * HEAD : (j + 1) * HEAD]
            weights = jnp.where(allowed, jnp.exp(dot(q, keys, 1, 1) * scale), 0.0)
            probs = weights / jnp.sum(weights, axis=-1, keepdims=True)
            low = probs.astype(BF16)
            att[e, :, j * HEAD : (j + 1) * HEAD] = dot(low, values, 1, 0).astype(BF16)
            gv = gv + dot(low, g, 0, 0)
            gp = dot(g, values, 1, 1)
            rdot = jnp.sum(gp * probs, axis=-1, keepdims=True)
            gs = (probs * (gp - rdot) * scale).astype(BF16)
            Gq[e, zl, :, j * HEAD : (j + 1) * HEAD] = unrope(dot(gs, keys, 1, 0)).astype(BF16)
            gk = gk + dot(gs, q, 0, 0)
        gk = unrope(gk)
        for i, v in enumerate((gk[:, :64], gk[:, 64:], gv[:, :64], gv[:, 64:])):
            v = pack(v)
            gfp[e, i] = v
            gsb[e, i] = v.astype(BF16)
        for o in (1, 2, 3):
            send(gsb.at[e, up(zh, o)], grb.at[e, o - 1], gr[e][o - 1], zto[o])
    save_att = local(att.at[0], att_out.at[0])
    send(att.at[1], att_out.at[1], ar[0], mirror)

    xr = [(rr.at[take("r")], rr.at[take("r")]) for e in (0, 1)]
    for e in (0, 1):
        send(Gq.at[e, zl], Gq.at[e, zl], xr[e][0], partner)
    for e in (0, 1):
        total = gfp[e, zh]
        for o in (1, 2, 3):
            arrived(grb.at[e, o - 1], gr[e][o - 1], zfrom[o])
            total = total + grb[e, o - 1].astype(F32)
        Gkvp[e, zl] = total.astype(BF16)
        send(Gkvp.at[e, zl], Gkvp.at[e, zl], xr[e][1], partner)
    for e in (0, 1):
        arrived(Gq.at[e, zflip], xr[e][0], partner)
        arrived(Gkvp.at[e, zflip], xr[e][1], partner)
        for d in (0, 1):
            Gkv[e, d] = unpack(Gkvp[e, d]).astype(BF16)

    def term(f, e, s):
        xs, zs = s
        d = lax.div(xs, 2)
        rows = pl.ds(block(xs, zs), FEAT)
        return dot(Gq[e, d, part(f, None)], Wq[rows, :], 1, 1) + dot(Gkv[e, d, part(f, None)], Wkv[rows, :], 1, 1)

    BACK = (2, 1, -1, 0)
    sem = {}

    def rsem(*key):
        if key not in sem:
            sem[key] = rr.at[take("r")]
        return sem[key]

    def raxes(f):
        B, A, b, a = axes(f)
        return A, B, a, b

    def rslot(f, a, b):
        A, B, _, _ = raxes(f)
        return slot(A, a, b)

    def scatter_far(e, i):
        k = BACK[i]
        for f in flows:
            A, B, a, b = raxes(f)
            sd[e, i, part(f, None)] = term(f, e, rslot(f, up(a, 2), up(b, k))).astype(BF16)
            for half, sign in ((0, 1), (1, -1)):
                send(sd.at[e, i, part(f, half)], rd.at[e, i, part(f, half)], rsem("d", f, e, i, half), neighbour[(A, sign)])

    def add_half(f, v, ref, half):
        n = FLOWS[f][1] // 2
        other = ref.astype(F32)
        if half == 0:
            return jnp.concatenate([v[:n] + other, v[n:]], axis=0)
        return jnp.concatenate([v[:n], v[n:] + other], axis=0)

    def scatter_near(e, i):
        k = BACK[i]
        for f in flows:
            A, B, a, b = raxes(f)
            for half, sign, out, into in ((0, 1, sp, rp), (1, -1, sm, rm)):
                v = term(f, e, rslot(f, up(a, sign), up(b, k)))
                arrived(rd.at[e, i, part(f, half)], rsem("d", f, e, i, half), neighbour[(A, -sign)])
                v = add_half(f, v, rd[e, i, part(f, half)], half)
                out[e, i, part(f, None)] = v.astype(BF16)
                send(out.at[e, i, part(f, None)], into.at[e, i, part(f, None)], rsem("n", f, e, i, half), neighbour[(A, sign)])

    def scatter_own(e, i):
        k = BACK[i]
        for f in flows:
            A, B, a, b = raxes(f)
            rows = part(f, None)
            v = term(f, e, rslot(f, a, up(b, k)))
            for half, sign, into in ((0, 1, rp), (1, -1, rm)):
                arrived(into.at[e, i, rows], rsem("n", f, e, i, half), neighbour[(A, -sign)])
                v = v + into[e, i, rows].astype(F32)
            if k == 2:
                zsd[e, rows] = v.astype(BF16)
                for half, sign in ((0, 1), (1, -1)):
                    send(zsd.at[e, part(f, half)], zrd.at[e, part(f, half)], rsem("zd", f, e, half), neighbour[(B, sign)])
            elif k in (1, -1):
                half, out, into = (0, zsp, zrp) if k == 1 else (1, zsm, zrm)
                arrived(zrd.at[e, part(f, half)], rsem("zd", f, e, half), neighbour[(B, -k)])
                v = add_half(f, v, zrd[e, part(f, half)], half)
                out[e, rows] = v.astype(BF16)
                send(out.at[e, rows], into.at[e, rows], rsem("zn", f, e, half), neighbour[(B, k)])
            else:
                for half, sign, into in ((0, 1, zrp), (1, -1, zrm)):
                    arrived(into.at[e, rows], rsem("zn", f, e, half), neighbour[(B, -sign)])
                    v = v + into[e, rows].astype(F32)
                fin[e, rows] = v.astype(BF16)

    save = []

    def weight_grads(i):
        bit, zs = i // 4, i % 4
        tq = jnp.zeros((FEAT, TOK), F32)
        tkv = jnp.zeros((FEAT, 64), F32)
        for d in (0, 1):
            xs = 2 * d + lax.rem(bit + d + zl, 2)
            for e in (0, 1):
                xb = X[e, xs, zs]
                tq = tq + dot(xb, Gq[e, d], 0, 0)
                tkv = tkv + dot(xb, Gkv[e, d], 0, 0)
        wgq[i] = tq
        wgkv[i] = tkv
        save.append(local(wgq.at[i], gq_out.at[pl.ds(i * FEAT, FEAT)]))
        save.append(local(wgkv.at[i], gkv_out.at[pl.ds(i * FEAT, FEAT)]))

    for i in range(4):
        for e in (0, 1):
            scatter_far(e, i)
    for i in range(4):
        for e in (0, 1):
            scatter_near(e, i)
        weight_grads(i)
    for i in range(4):
        weight_grads(4 + i)
        for e in (0, 1):
            scatter_own(e, i)

    f1r = rr.at[take("r")]
    send(fin.at[1], hg_out.at[1], f1r, swap1)
    f0s, f0r, f0l = ss.at[take("s")], rr.at[take("r")], ls.at[take("l")]

    @pl.when(own)
    def _():
        copy = pltpu.make_async_copy(fin.at[0], hg_out.at[0], f0l)
        copy.start()
        copy.wait()

    @pl.when(jnp.logical_not(own))
    def _():
        copy = pltpu.make_async_remote_copy(
            src_ref=fin.at[0], dst_ref=hg_out.at[0], send_sem=f0s, recv_sem=f0r, device_id=swap0, device_id_type=MESH
        )
        copy.start()
        copy.wait()

    arrived(hg_out.at[1], f1r, swap1)
    arrived(att_out.at[1], ar[0], mirror)
    save_att.wait()
    for copy in save:
        copy.wait()
    for copy in pending:
        copy.wait_send()


def rope_tables():
    freqs = 10000.0 ** (-2.0 * np.arange(HEAD // 2) / HEAD)
    angles = np.arange(TOK, dtype=np.float32)[:, None] * freqs.astype(np.float32)[None, :]
    cosine, sine = np.cos(angles), np.sin(angles)
    return (
        np.concatenate([cosine, cosine], 1).astype(np.float32),
        np.concatenate([-sine, sine], 1).astype(np.float32),
    )


def body(hidden, query_weight, keyval_weight, doc_ids, cotangent):
    cosf, sinf = rope_tables()
    anywhere = pl.BlockSpec(memory_space=pl.ANY)
    vmem = pl.BlockSpec(memory_space=pltpu.VMEM)
    V = pltpu.VMEM
    big = V((2, 4, TOK, FEAT), BF16)
    mid = V((2, TOK, FEAT), BF16)
    nf = len(FLOWS)
    scratch = [
        V((2, 4, 4, TOK, FEAT), BF16),
        V((4096, 256), BF16), V((4096, 64), BF16),
        V((2, TOK, 256), BF16), V((1, TOK), jnp.int32),
        V((2, 2, TOK, 256), F32), V((2, 2, TOK, 64), F32),
        V((2, TOK, 256), BF16), V((2, 128, 128), BF16), V((2, TOK, 256), BF16), V((2, 128, 128), BF16),
        V((2, 4, 128, 128), BF16),
        V((2, 4, 128, 128), F32), V((2, 4, 128, 128), BF16), V((2, 3, 128, 128), BF16),
        V((2, 2, TOK, 256), BF16), V((2, 2, 128, 128), BF16), V((2, 2, TOK, 64), BF16),
        V((2, 2, TOK, HEAD), BF16), V((2, TOK, HEAD), BF16), V((2, TOK, HEAD), BF16),
        V((2, TOK, 256), BF16),
        big, big, big, big, big, big,
        mid, mid, mid, mid, mid, mid, mid,
        V((8, FEAT, 256), F32), V((8, FEAT, 64), F32),
        pltpu.SemaphoreType.DMA((64 + 96 * nf,)),
        pltpu.SemaphoreType.DMA((48 + 48 * nf,)),
        pltpu.SemaphoreType.DMA((nf, 2, 4, 4, 2)),
        pltpu.SemaphoreType.DMA((32,)),
    ]
    att, hg, gq, gkv = pl.pallas_call(
        kernel,
        out_shape=(
            jax.ShapeDtypeStruct((2, TOK, 256), BF16),
            jax.ShapeDtypeStruct((2, TOK, FEAT), BF16),
            jax.ShapeDtypeStruct((4096, 256), F32),
            jax.ShapeDtypeStruct((4096, 64), F32),
        ),
        in_specs=[anywhere, anywhere, anywhere, vmem, anywhere, vmem, vmem],
        out_specs=(anywhere,) * 4,
        scratch_shapes=scratch,
        compiler_params=pltpu.CompilerParams(
            collective_id=0, has_side_effects=True, vmem_limit_bytes=60 * 2**20
        ),
    )(hidden[0], query_weight[0], keyval_weight[0], doc_ids[0], cotangent[0], cosf, sinf)
    return att[None], hg[None], gq[None], gkv[None]


def solution(mesh):
    sharded = P("pipe", None, "dp", "tensor")
    return jax.shard_map(
        body,
        mesh=mesh,
        in_specs=(sharded, sharded, sharded, P("pipe", None, "dp", None), sharded),
        out_specs=(sharded, sharded, P("pipe", "dp", "tensor"), P("pipe", "dp", "tensor")),
        check_vma=False,
    )
```

```python
import jax
import jax.numpy as jnp
import numpy as np
from jax import lax
from jax.experimental import pallas as pl
from jax.experimental.pallas import tpu as pltpu
from jax.sharding import PartitionSpec as P

MESH = pl.DeviceIdType.MESH
HEAD = 128
TOK = 256
FEAT = 512
F32 = jnp.float32
BF16 = jnp.bfloat16
FLOWS = ((0, 192, "z"), (192, 64, "x"))


def dot(a, b, ca, cb):
    return lax.dot_general(a, b, (((ca,), (cb,)), ((), ())), preferred_element_type=F32)


def pack(v):
    return jnp.concatenate([v[: TOK // 2], v[TOK // 2 :]], axis=1)


def unpack(v):
    v = v.astype(F32)
    return jnp.concatenate([v[:, :64], v[:, 64:]], axis=0)


def kernel(
    hid, wq, wkv, doc, cot, cosf, sinf,
    att_out, hg_out, gq_out, gkv_out,
    X, Wq, Wkv, C, docs, Pq, Pkv, sPq, sPkv, rPq, rPkv, KV, gfp, gsb, grb, Gq, Gkvp, Gkv, Qb, att,
    sd, sp, sm, rd, rp, rm, zsd, zsp, zsm, zrd, zrp, zrm, fin, wgq, wgkv,
    ss, rr, ra, ls,
):
    pipe, tens, zl = lax.axis_index("pipe"), lax.axis_index("tensor"), lax.axis_index("dp")
    x, zh = lax.div(tens, 4), lax.rem(tens, 4)
    y, c = lax.div(pipe, 2), lax.rem(pipe, 2)
    own = lax.div(x, 2) == zl

    def dev(x, y, zh, zl, c):
        return {"pipe": y * 2 + c, "tensor": x * 4 + zh, "dp": zl}

    def up(v, k):
        return lax.rem(v + k + 4, 4)

    zflip = 1 - zl
    neighbour = {
        ("x", 1): dev(up(x, 1), y, zh, zl, c),
        ("x", -1): dev(up(x, -1), y, zh, zl, c),
        ("z", 1): dev(x, y, up(zh, 1), zl, c),
        ("z", -1): dev(x, y, up(zh, -1), zl, c),
        ("z", 2): dev(x, y, up(zh, 2), zl, c),
    }
    partner = dev(x, y, zh, zflip, c)
    mirror = dev(x, 3 - y, zh, zl, 1 - c)
    swap0 = dev(3 - x, y, zh, zflip, c)
    swap1 = dev(jnp.where(own, x, 3 - x), 3 - y, zh, jnp.where(own, zl, zflip), 1 - c)

    count = {"s": 0, "r": 0, "l": 0}
    pending = []
    save = []

    def take(kind):
        count[kind] += 1
        return count[kind] - 1

    def send(src, dst, rsem, to):
        copy = pltpu.make_async_remote_copy(
            src_ref=src, dst_ref=dst, send_sem=ss.at[take("s")], recv_sem=rsem, device_id=to, device_id_type=MESH
        )
        copy.start()
        pending.append(copy)

    def arrived(dst, rsem, frm):
        pltpu.make_async_remote_copy(
            src_ref=dst, dst_ref=dst, send_sem=ss.at[0], recv_sem=rsem, device_id=frm, device_id_type=MESH
        ).wait_recv()

    def local(src, dst):
        copy = pltpu.make_async_copy(src, dst, ls.at[take("l")])
        copy.start()
        return copy

    barrier = pltpu.get_barrier_semaphore()
    greet0 = dev(
        jnp.where(own, x, 3 - x), jnp.where(own, 3 - y, y), zh, jnp.where(own, zl, zflip), jnp.where(own, 1 - c, c)
    )
    for to in list(neighbour.values()) + [partner, mirror, swap1, greet0]:
        pl.semaphore_signal(barrier, inc=1, device_id=to, device_id_type=MESH)
    pl.semaphore_wait(barrier, 9)

    s0s, s0r, s0l = ss.at[take("s")], rr.at[take("r")], ls.at[take("l")]

    def keep(src, dst, start):
        copy = pltpu.make_async_copy(src, dst, s0l)
        copy.start() if start else copy.wait()

    def swap(src, dst, start):
        copy = pltpu.make_async_remote_copy(
            src_ref=src, dst_ref=dst, send_sem=s0s, recv_sem=s0r, device_id=swap0, device_id_type=MESH
        )
        copy.start() if start else copy.wait()

    def stage0(start):
        @pl.when(own)
        def _():
            keep(hid.at[0], X.at[0, x, zh], start)

        @pl.when(jnp.logical_not(own))
        def _():
            swap(hid.at[0], X.at[0, 3 - x, zh], start)

    s1r, cr, dr = rr.at[take("r")], rr.at[take("r")], rr.at[take("r")]
    stage0(True)
    send(hid.at[1], X.at[1, jnp.where(own, x, 3 - x), zh], s1r, swap1)
    load_wq = local(wq.at[0], Wq)
    load_wkv = local(wkv.at[0], Wkv)
    load_c = local(cot.at[0], C.at[0])
    send(cot.at[1], C.at[1], cr, mirror)
    send(doc.at[1], docs, dr, mirror)
    Pq[...] = jnp.zeros_like(Pq)
    Pkv[...] = jnp.zeros_like(Pkv)

    def block(xs, zs):
        bit = lax.rem(lax.rem(xs, 2) + lax.div(xs, 2) + zl, 2)
        return pl.multiple_of((bit * 4 + zs) * FEAT, FEAT)

    def project(e, xs, zs):
        d = lax.div(xs, 2)
        rows = pl.ds(block(xs, zs), FEAT)
        xb = X[e, xs, zs]
        Pq[e, d] += dot(xb, Wq[rows, :], 1, 0)
        Pkv[e, d] += dot(xb, Wkv[:, rows], 1, 1)

    pos = {"x": x, "z": zh}

    def slot(first, a, b):
        return (a, b) if first == "x" else (b, a)

    def part(flow, half):
        r0, n, _ = FLOWS[flow]
        if half is None:
            return pl.ds(r0, n)
        return pl.ds(r0 + half * (n // 2), n // 2)

    def fwd(f, e, s, half, axis, sign):
        ref = X.at[e, s[0], s[1], part(f, half)]
        send(ref, ref, ra.at[f, e, s[0], s[1], half or 0], neighbour[(axis, sign)])

    def got(f, e, s, half, axis, sign):
        ref = X.at[e, s[0], s[1], part(f, half)]
        arrived(ref, ra.at[f, e, s[0], s[1], half or 0], neighbour[(axis, sign)])

    def axes(f):
        first = FLOWS[f][2]
        second = "z" if first == "x" else "x"
        return first, second, pos[first], pos[second]

    flows = range(len(FLOWS))

    def gather_first(e):
        for f in flows:
            A, B, a, b = axes(f)
            s = slot(A, a, b)
            fwd(f, e, s, None, A, 1)
            fwd(f, e, s, None, A, -1)
            fwd(f, e, s, None, B, 1)
            fwd(f, e, s, None, B, -1)

    def gather_second(e):
        for f in flows:
            A, B, a, b = axes(f)
            s = slot(A, up(a, -1), b)
            got(f, e, s, None, A, -1)
            fwd(f, e, s, 0, A, 1)
            fwd(f, e, s, None, B, 1)
            fwd(f, e, s, None, B, -1)
            s = slot(A, up(a, 1), b)
            got(f, e, s, None, A, 1)
            fwd(f, e, s, 1, A, -1)
            fwd(f, e, s, None, B, 1)
            fwd(f, e, s, None, B, -1)

    def gather_third(e):
        for f in flows:
            A, B, a, b = axes(f)
            s = slot(A, up(a, 2), b)
            got(f, e, s, 0, A, -1)
            got(f, e, s, 1, A, 1)
            fwd(f, e, s, None, B, 1)
            fwd(f, e, s, None, B, -1)

    def gather_near(e, k):
        for f in flows:
            A, B, a, b = axes(f)
            s = slot(A, up(a, k), up(b, -1))
            got(f, e, s, None, B, -1)
            fwd(f, e, s, 0, B, 1)
            s = slot(A, up(a, k), up(b, 1))
            got(f, e, s, None, B, 1)
            fwd(f, e, s, 1, B, -1)

    def gather_far(e, k):
        for f in flows:
            A, B, a, b = axes(f)
            s = slot(A, up(a, k), up(b, 2))
            got(f, e, s, 0, B, -1)
            got(f, e, s, 1, B, 1)

    ORDER = (0, -1, 1, 2)

    def project_near(e):
        for i in (-1, 0, 1):
            for k in (-1, 0, 1):
                project(e, up(x, i), up(zh, k))

    def project_far(e):
        for i in ORDER:
            for k in ORDER:
                if i == 2 or k == 2:
                    project(e, up(x, i), up(zh, k))

    cosw, sinw = cosf[...], sinf[...]

    def rope(v):
        return v * cosw + pltpu.roll(v, 64, 1) * sinw

    def unrope(v):
        return v * cosw - pltpu.roll(v, 64, 1) * sinw

    zto = {1: neighbour[("z", 1)], 2: neighbour[("z", 2)], 3: neighbour[("z", -1)]}
    zfrom = {1: neighbour[("z", -1)], 2: neighbour[("z", 2)], 3: neighbour[("z", 1)]}
    pr = [(rr.at[take("r")], rr.at[take("r")]) for e in (0, 1)]
    kvr = [[rr.at[take("r")] for o in (1, 2, 3)] for e in (0, 1)]
    gr = [[rr.at[take("r")] for o in (1, 2, 3)] for e in (0, 1)]
    xr = [(rr.at[take("r")], rr.at[take("r")]) for e in (0, 1)]
    ar = rr.at[take("r")]
    scale = HEAD**-0.5

    def send_partial(e):
        sPkv[e] = pack(Pkv[e, zflip]).astype(BF16)
        send(sPkv.at[e], rPkv.at[e], pr[e][1], partner)
        sPq[e] = Pq[e, zflip].astype(BF16)
        send(sPq.at[e], rPq.at[e], pr[e][0], partner)

    def send_kv(e):
        arrived(rPkv.at[e], pr[e][1], partner)
        piece = pack(Pkv[e, zl]) + rPkv[e].astype(F32)
        KV[e, zh] = piece.astype(BF16)
        for o in (1, 2, 3):
            send(KV.at[e, zh], KV.at[e, zh], kvr[e][o - 1], zto[o])
        arrived(rPq.at[e], pr[e][0], partner)
        q = Pq[e, zl] + rPq[e].astype(F32)
        Qb[e, 0] = rope(q[:, :HEAD]).astype(BF16)
        Qb[e, 1] = rope(q[:, HEAD:]).astype(BF16)

    def attend(e):
        if e == 0:
            load_c.wait()
        else:
            arrived(C.at[1], cr, mirror)
            arrived(docs, dr, mirror)
        row = lax.broadcasted_iota(jnp.int32, (TOK, TOK), 0)
        col = lax.broadcasted_iota(jnp.int32, (TOK, TOK), 1)
        ids = doc[0] if e == 0 else docs[...]
        wide = jnp.broadcast_to(ids.astype(F32), (TOK, TOK))
        allowed = (wide == wide.T) & (col <= row)
        for o in (1, 2, 3):
            arrived(KV.at[e, up(zh, -o)], kvr[e][o - 1], zfrom[o])
        kraw = jnp.concatenate([unpack(KV[e, 0]), unpack(KV[e, 1])], axis=1)
        keys = rope(kraw).astype(BF16)
        values = jnp.concatenate([unpack(KV[e, 2]), unpack(KV[e, 3])], axis=1).astype(BF16)
        gk = jnp.zeros((TOK, HEAD), F32)
        gv = jnp.zeros((TOK, HEAD), F32)
        for j in (0, 1):
            q = Qb[e, j]
            g = C[e, :, j * HEAD : (j + 1) * HEAD]
            weights = jnp.where(allowed, jnp.exp(dot(q, keys, 1, 1) * scale), 0.0)
            probs = weights / jnp.sum(weights, axis=-1, keepdims=True)
            low = probs.astype(BF16)
            att[e, :, j * HEAD : (j + 1) * HEAD] = dot(low, values, 1, 0).astype(BF16)
            gv = gv + dot(low, g, 0, 0)
            gp = dot(g, values, 1, 1)
            rdot = jnp.sum(gp * probs, axis=-1, keepdims=True)
            gs = (probs * (gp - rdot) * scale).astype(BF16)
            Gq[e, zl, :, j * HEAD : (j + 1) * HEAD] = unrope(dot(gs, keys, 1, 0)).astype(BF16)
            gk = gk + dot(gs, q, 0, 0)
        gk = unrope(gk)
        for i, v in enumerate((gk[:, :64], gk[:, 64:], gv[:, :64], gv[:, 64:])):
            v = pack(v)
            gfp[e, i] = v
            gsb[e, i] = v.astype(BF16)
        for o in (1, 2, 3):
            send(gsb.at[e, up(zh, o)], grb.at[e, o - 1], gr[e][o - 1], zto[o])
        send(Gq.at[e, zl], Gq.at[e, zl], xr[e][0], partner)
        if e == 0:
            save.append(local(att.at[0], att_out.at[0]))
        else:
            send(att.at[1], att_out.at[1], ar, mirror)

    def send_gkv(e):
        total = gfp[e, zh]
        for o in (1, 2, 3):
            arrived(grb.at[e, o - 1], gr[e][o - 1], zfrom[o])
            total = total + grb[e, o - 1].astype(F32)
        Gkvp[e, zl] = total.astype(BF16)
        send(Gkvp.at[e, zl], Gkvp.at[e, zl], xr[e][1], partner)

    def take_g(e):
        arrived(Gq.at[e, zflip], xr[e][0], partner)
        arrived(Gkvp.at[e, zflip], xr[e][1], partner)
        for d in (0, 1):
            Gkv[e, d] = unpack(Gkvp[e, d]).astype(BF16)

    def term(f, e, s):
        xs, zs = s
        d = lax.div(xs, 2)
        rows = pl.ds(block(xs, zs), FEAT)
        return dot(Gq[e, d, part(f, None)], Wq[rows, :], 1, 1) + dot(Gkv[e, d, part(f, None)], Wkv[:, rows], 1, 0)

    BACK = (2, 1, -1, 0)
    sem = {}

    def rsem(*key):
        if key not in sem:
            sem[key] = rr.at[take("r")]
        return sem[key]

    def raxes(f):
        B, A, b, a = axes(f)
        return A, B, a, b

    def rslot(f, a, b):
        A, B, _, _ = raxes(f)
        return slot(A, a, b)

    def scatter_far(e, i):
        k = BACK[i]
        for f in flows:
            A, B, a, b = raxes(f)
            sd[e, i, part(f, None)] = term(f, e, rslot(f, up(a, 2), up(b, k))).astype(BF16)
            for half, sign in ((0, 1), (1, -1)):
                send(sd.at[e, i, part(f, half)], rd.at[e, i, part(f, half)], rsem("d", f, e, i, half), neighbour[(A, sign)])

    def add_half(f, v, ref, half):
        n = FLOWS[f][1] // 2
        other = ref.astype(F32)
        if half == 0:
            return jnp.concatenate([v[:n] + other, v[n:]], axis=0)
        return jnp.concatenate([v[:n], v[n:] + other], axis=0)

    def scatter_near(e, i):
        k = BACK[i]
        for f in flows:
            A, B, a, b = raxes(f)
            for half, sign, out, into in ((0, 1, sp, rp), (1, -1, sm, rm)):
                v = term(f, e, rslot(f, up(a, sign), up(b, k)))
                arrived(rd.at[e, i, part(f, half)], rsem("d", f, e, i, half), neighbour[(A, -sign)])
                v = add_half(f, v, rd[e, i, part(f, half)], half)
                out[e, i, part(f, None)] = v.astype(BF16)
                send(out.at[e, i, part(f, None)], into.at[e, i, part(f, None)], rsem("n", f, e, i, half), neighbour[(A, sign)])

    def scatter_own(e, i):
        k = BACK[i]
        for f in flows:
            A, B, a, b = raxes(f)
            rows = part(f, None)
            v = term(f, e, rslot(f, a, up(b, k)))
            for half, sign, into in ((0, 1, rp), (1, -1, rm)):
                arrived(into.at[e, i, rows], rsem("n", f, e, i, half), neighbour[(A, -sign)])
                v = v + into[e, i, rows].astype(F32)
            if k == 2:
                zsd[e, rows] = v.astype(BF16)
                for half, sign in ((0, 1), (1, -1)):
                    send(zsd.at[e, part(f, half)], zrd.at[e, part(f, half)], rsem("zd", f, e, half), neighbour[(B, sign)])
            elif k in (1, -1):
                half, out, into = (0, zsp, zrp) if k == 1 else (1, zsm, zrm)
                arrived(zrd.at[e, part(f, half)], rsem("zd", f, e, half), neighbour[(B, -k)])
                v = add_half(f, v, zrd[e, part(f, half)], half)
                out[e, rows] = v.astype(BF16)
                send(out.at[e, rows], into.at[e, rows], rsem("zn", f, e, half), neighbour[(B, k)])
            else:
                for half, sign, into in ((0, 1, zrp), (1, -1, zrm)):
                    arrived(into.at[e, rows], rsem("zn", f, e, half), neighbour[(B, -sign)])
                    v = v + into[e, rows].astype(F32)
                fin[e, rows] = v.astype(BF16)

    def weight_grads(i):
        bit, zs = i // 4, i % 4
        tq = jnp.zeros((FEAT, TOK), F32)
        tkv = jnp.zeros((64, FEAT), F32)
        for d in (0, 1):
            xs = 2 * d + lax.rem(bit + d + zl, 2)
            for e in (0, 1):
                xb = X[e, xs, zs]
                tq = tq + dot(xb, Gq[e, d], 0, 0)
                tkv = tkv + dot(Gkv[e, d], xb, 0, 0)
        wgq[i] = tq.astype(BF16)
        wgkv[i] = tkv
        save.append(local(wgq.at[i], gq_out.at[pl.ds(i * FEAT, FEAT)]))
        save.append(local(wgkv.at[i], gkv_out.at[:, pl.ds(i * FEAT, FEAT)]))

    def fars(e):
        for i in range(4):
            scatter_far(e, i)

    def nears(e):
        for i in range(4):
            scatter_near(e, i)

    stage0(False)
    gather_first(0)
    load_wq.wait()
    load_wkv.wait()
    gather_second(0)
    gather_third(0)
    arrived(X.at[1, x, zh], s1r, swap1)
    gather_first(1)
    for k in ORDER:
        gather_near(0, k)
    gather_second(1)
    gather_third(1)
    project_near(0)
    for k in ORDER:
        gather_far(0, k)
    project_far(0)
    send_partial(0)
    gather_near(1, 0)
    gather_near(1, -1)
    send_kv(0)
    gather_near(1, 1)
    gather_near(1, 2)
    attend(0)
    project_near(1)
    send_gkv(0)
    for k in ORDER:
        gather_far(1, k)
    project_far(1)
    send_partial(1)
    take_g(0)
    fars(0)
    send_kv(1)
    nears(0)
    attend(1)
    scatter_own(0, 0)
    send_gkv(1)
    scatter_own(0, 1)
    take_g(1)
    fars(1)
    scatter_own(0, 2)
    scatter_own(0, 3)
    f1r = rr.at[take("r")]

    def final0(start):
        @pl.when(own)
        def _():
            keep(fin.at[0], hg_out.at[0], start)

        @pl.when(jnp.logical_not(own))
        def _():
            swap(fin.at[0], hg_out.at[0], start)

    final0(True)
    for i in range(4):
        weight_grads(i)
    nears(1)
    for i in range(4):
        weight_grads(4 + i)
    for i in range(4):
        scatter_own(1, i)
    send(fin.at[1], hg_out.at[1], f1r, swap1)
    final0(False)
    arrived(hg_out.at[1], f1r, swap1)
    arrived(att_out.at[1], ar, mirror)
    for copy in save:
        copy.wait()
    for copy in pending:
        copy.wait_send()


def rope_tables():
    freqs = 10000.0 ** (-2.0 * np.arange(HEAD // 2) / HEAD)
    angles = np.arange(TOK, dtype=np.float32)[:, None] * freqs.astype(np.float32)[None, :]
    cosine, sine = np.cos(angles), np.sin(angles)
    return (
        np.concatenate([cosine, cosine], 1).astype(np.float32),
        np.concatenate([-sine, sine], 1).astype(np.float32),
    )


def body(hidden, query_weight, keyval_weight, doc_ids, cotangent):
    cosf, sinf = rope_tables()
    anywhere = pl.BlockSpec(memory_space=pl.ANY)
    vmem = pl.BlockSpec(memory_space=pltpu.VMEM)
    V = pltpu.VMEM
    big = V((2, 4, TOK, FEAT), BF16)
    mid = V((2, TOK, FEAT), BF16)
    nf = len(FLOWS)
    scratch = [
        V((2, 4, 4, TOK, FEAT), BF16),
        V((4096, 256), BF16), V((64, 4096), BF16),
        V((2, TOK, 256), BF16), V((1, TOK), jnp.int32),
        V((2, 2, TOK, 256), F32), V((2, 2, TOK, 64), F32),
        V((2, TOK, 256), BF16), V((2, 128, 128), BF16), V((2, TOK, 256), BF16), V((2, 128, 128), BF16),
        V((2, 4, 128, 128), BF16),
        V((2, 4, 128, 128), F32), V((2, 4, 128, 128), BF16), V((2, 3, 128, 128), BF16),
        V((2, 2, TOK, 256), BF16), V((2, 2, 128, 128), BF16), V((2, 2, TOK, 64), BF16),
        V((2, 2, TOK, HEAD), BF16),
        V((2, TOK, 256), BF16),
        big, big, big, big, big, big,
        mid, mid, mid, mid, mid, mid, mid,
        V((8, FEAT, 256), BF16), V((8, 64, FEAT), F32),
        pltpu.SemaphoreType.DMA((64 + 96 * nf,)),
        pltpu.SemaphoreType.DMA((48 + 48 * nf,)),
        pltpu.SemaphoreType.DMA((nf, 2, 4, 4, 2)),
        pltpu.SemaphoreType.DMA((32,)),
    ]
    att, hg, gq, gkv = pl.pallas_call(
        kernel,
        out_shape=(
            jax.ShapeDtypeStruct((2, TOK, 256), BF16),
            jax.ShapeDtypeStruct((2, TOK, FEAT), BF16),
            jax.ShapeDtypeStruct((4096, 256), BF16),
            jax.ShapeDtypeStruct((64, 4096), F32),
        ),
        in_specs=[anywhere, anywhere, anywhere, vmem, anywhere, vmem, vmem],
        out_specs=(anywhere,) * 4,
        scratch_shapes=scratch,
        compiler_params=pltpu.CompilerParams(
            collective_id=0, has_side_effects=True, vmem_limit_bytes=60 * 2**20
        ),
    )(hidden[0], query_weight[0], keyval_weight[0].swapaxes(1, 2), doc_ids[0], cotangent[0], cosf, sinf)
    return att[None], hg[None], gq.astype(F32)[None], gkv.T[None]


def solution(mesh):
    sharded = P("pipe", None, "dp", "tensor")
    return jax.shard_map(
        body,
        mesh=mesh,
        in_specs=(sharded, sharded, sharded, P("pipe", None, "dp", None), sharded),
        out_specs=(sharded, sharded, P("pipe", "dp", "tensor"), P("pipe", "dp", "tensor")),
        check_vma=False,
    )
```

```python
import jax
import jax.numpy as jnp
import numpy as np
from jax import lax
from jax.experimental import pallas as pl
from jax.experimental.pallas import tpu as pltpu
from jax.sharding import PartitionSpec as P

MESH = pl.DeviceIdType.MESH
HEAD = 128
TOK = 256
FEAT = 512
F32 = jnp.float32
BF16 = jnp.bfloat16
QUARTER = 2048


def dot(a, b, ca, cb):
    return lax.dot_general(a, b, (((ca,), (cb,)), ((), ())), preferred_element_type=F32)


def pack(v):
    return jnp.concatenate([v[: TOK // 2], v[TOK // 2 :]], axis=1)


def unpack(v):
    v = v.astype(F32)
    return jnp.concatenate([v[:, :64], v[:, 64:]], axis=0)


def kernel(
    hid, wq, wkv, doc, cot, cosf, sinf,
    att_out, hg_out, gq_out, gkv_out,
    X, Wq, Wkv, C, docs, Pq, Pkv, PkvP, sPq, sPkv, rPq, rPkv, KV, gfp, gsb, grb, Gq, Gkvp, Gkv, Qb, att,
    sd, rd, zsd, zsp, zsm, zrd, zrp, zrm, fin, wgq, wgkv,
    ss, rr, ra, ls,
):
    pipe, tens, zl = lax.axis_index("pipe"), lax.axis_index("tensor"), lax.axis_index("dp")
    x, zh = lax.div(tens, 4), lax.rem(tens, 4)
    y, c = lax.div(pipe, 2), lax.rem(pipe, 2)
    own = lax.div(x, 2) == zl

    def dev(x, y, zh, zl, c):
        return {"pipe": y * 2 + c, "tensor": x * 4 + zh, "dp": zl}

    def up(v, k):
        return lax.rem(v + k + 4, 4)

    zflip = 1 - zl
    xb = lax.rem(x, 2)
    xpair = x + 1 - 2 * xb
    held = lax.div(x, 2)
    qb = lax.rem(xb + held + zl, 2)
    neighbour = {
        1: dev(x, y, up(zh, 1), zl, c),
        -1: dev(x, y, up(zh, -1), zl, c),
        2: dev(x, y, up(zh, 2), zl, c),
    }
    across = dev(3 - x, y, zh, zl, c)
    pair = dev(xpair, y, zh, zl, c)
    square = (pair, dev(x, y, zh, zflip, c), dev(xpair, y, zh, zflip, c))
    mirror = dev(x, 3 - y, zh, zl, 1 - c)
    swap0 = dev(3 - x, y, zh, zflip, c)
    swap1 = dev(jnp.where(own, x, 3 - x), 3 - y, zh, jnp.where(own, zl, zflip), 1 - c)

    count = {"s": 0, "r": 0, "l": 0}
    pending = []
    save = []

    def take(kind):
        count[kind] += 1
        return count[kind] - 1

    def send(src, dst, rsem, to):
        copy = pltpu.make_async_remote_copy(
            src_ref=src, dst_ref=dst, send_sem=ss.at[take("s")], recv_sem=rsem, device_id=to, device_id_type=MESH
        )
        copy.start()
        pending.append(copy)

    def arrived(dst, rsem, frm):
        pltpu.make_async_remote_copy(
            src_ref=dst, dst_ref=dst, send_sem=ss.at[0], recv_sem=rsem, device_id=frm, device_id_type=MESH
        ).wait_recv()

    def local(src, dst):
        copy = pltpu.make_async_copy(src, dst, ls.at[take("l")])
        copy.start()
        return copy

    barrier = pltpu.get_barrier_semaphore()
    greet0 = dev(
        jnp.where(own, x, 3 - x), jnp.where(own, 3 - y, y), zh, jnp.where(own, zl, zflip), jnp.where(own, 1 - c, c)
    )
    for to in list(neighbour.values()) + [across, mirror, swap1, greet0] + list(square):
        pl.semaphore_signal(barrier, inc=1, device_id=to, device_id_type=MESH)
    pl.semaphore_wait(barrier, 10)

    s0s, s0r, s0l = ss.at[take("s")], rr.at[take("r")], ls.at[take("l")]

    def keep(src, dst, start):
        copy = pltpu.make_async_copy(src, dst, s0l)
        copy.start() if start else copy.wait()

    def swap(src, dst, start):
        copy = pltpu.make_async_remote_copy(
            src_ref=src, dst_ref=dst, send_sem=s0s, recv_sem=s0r, device_id=swap0, device_id_type=MESH
        )
        copy.start() if start else copy.wait()

    def stage0(start):
        @pl.when(own)
        def _():
            keep(hid.at[0], X.at[0, held, zh], start)

        @pl.when(jnp.logical_not(own))
        def _():
            swap(hid.at[0], X.at[0, 1 - held, zh], start)

    s1r, cr, dr = rr.at[take("r")], rr.at[take("r")], rr.at[take("r")]
    stage0(True)
    send(hid.at[1], X.at[1, jnp.where(own, held, 1 - held), zh], s1r, swap1)
    mine = pl.ds(pl.multiple_of(qb * QUARTER, QUARTER), QUARTER)
    theirs = pl.ds(pl.multiple_of((1 - qb) * QUARTER, QUARTER), QUARTER)
    load_wq = local(wq.at[0, mine], Wq.at[xb])
    load_wkv = local(wkv.at[0, :, mine], Wkv.at[xb])
    wr = (rr.at[take("r")], rr.at[take("r")])
    send(wq.at[0, theirs], Wq.at[xb], wr[0], pair)
    send(wkv.at[0, :, theirs], Wkv.at[xb], wr[1], pair)
    load_c = local(cot.at[0], C.at[0])
    send(cot.at[1], C.at[1], cr, mirror)
    send(doc.at[1], docs, dr, mirror)
    Pq[...] = jnp.zeros_like(Pq)
    Pkv[...] = jnp.zeros_like(Pkv)

    def features(zs):
        return pl.ds(pl.multiple_of(zs * FEAT, FEAT), FEAT)

    def kv_weights(rows):
        return Wkv[:, :, rows].reshape(HEAD, FEAT)

    def project(e, d, zs):
        rows = features(zs)
        block = X[e, d, zs]
        for s in (0, 1):
            Pq[e, d, s] += dot(block, Wq[s, rows, :], 1, 0)
        Pkv[e, d] += dot(block, kv_weights(rows), 1, 1)

    HALF = (pl.ds(0, TOK // 2), pl.ds(TOK // 2, TOK // 2))

    def pass_on(e, k, half, sign):
        ref = X.at[e, held, up(zh, k)]
        if half is not None:
            ref = ref.at[HALF[half]]
        send(ref, ref, ra.at[e, held, up(zh, k), half or 0], neighbour[sign])

    def got(e, k, half, sign):
        ref = X.at[e, held, up(zh, k)]
        if half is not None:
            ref = ref.at[HALF[half]]
        arrived(ref, ra.at[e, held, up(zh, k), half or 0], neighbour[sign])

    def share(e, k):
        ref = X.at[e, held, up(zh, k)]
        send(ref, ref, ra.at[e, held, up(zh, k), 0], across)

    def shared(e, k):
        ref = X.at[e, 1 - held, up(zh, k)]
        arrived(ref, ra.at[e, 1 - held, up(zh, k), 0], across)

    def gather_first(e):
        pass_on(e, 0, None, 1)
        pass_on(e, 0, None, -1)
        share(e, 0)

    def gather_second(e):
        got(e, -1, None, -1)
        pass_on(e, -1, 0, 1)
        share(e, -1)
        got(e, 1, None, 1)
        pass_on(e, 1, 1, -1)
        share(e, 1)

    def gather_third(e):
        got(e, 2, 0, -1)
        got(e, 2, 1, 1)
        share(e, 2)

    ORDER = (0, -1, 1, 2)

    def project_held(e):
        for k in ORDER:
            project(e, held, up(zh, k))

    def project_shared(e):
        for k in ORDER:
            shared(e, k)
            project(e, 1 - held, up(zh, k))

    cosw, sinw = cosf[...], sinf[...]

    def rope(v):
        return v * cosw + pltpu.roll(v, 64, 1) * sinw

    def unrope(v):
        return v * cosw - pltpu.roll(v, 64, 1) * sinw

    zto = {1: neighbour[1], 2: neighbour[2], 3: neighbour[-1]}
    zfrom = {1: neighbour[-1], 2: neighbour[2], 3: neighbour[1]}

    def three():
        return [[rr.at[take("r")] for _ in range(3)] for e in (0, 1)]

    prq, prk, kvr, gr, xrq, xrk = three(), three(), three(), three(), three(), three()
    ar = rr.at[take("r")]
    members = ((zl, 1 - xb), (zflip, xb), (zflip, 1 - xb))
    scale = HEAD**-0.5

    def send_partial(e):
        for d in (0, 1):
            for s in (0, 1):
                PkvP[e, d, s] = pack(Pkv[e, d, :, 64 * s : 64 * s + 64])
        for i, (d, s) in enumerate(members):
            sPkv[e, i] = PkvP[e, d, s].astype(BF16)
            send(sPkv.at[e, i], rPkv.at[e, i], prk[e][i], square[i])
        for i, (d, s) in enumerate(members):
            sPq[e, i] = Pq[e, d, s].astype(BF16)
            send(sPq.at[e, i], rPq.at[e, i], prq[e][i], square[i])

    def send_kv(e):
        piece = PkvP[e, zl, xb]
        for i in range(3):
            arrived(rPkv.at[e, i], prk[e][i], square[i])
            piece = piece + rPkv[e, i].astype(F32)
        KV[e, zh] = piece.astype(BF16)
        for o in (1, 2, 3):
            send(KV.at[e, zh], KV.at[e, zh], kvr[e][o - 1], zto[o])
        q = Pq[e, zl, xb]
        for i in range(3):
            arrived(rPq.at[e, i], prq[e][i], square[i])
            q = q + rPq[e, i].astype(F32)
        Qb[e, 0] = rope(q[:, :HEAD]).astype(BF16)
        Qb[e, 1] = rope(q[:, HEAD:]).astype(BF16)

    def attend(e):
        if e == 0:
            load_c.wait()
        else:
            arrived(C.at[1], cr, mirror)
            arrived(docs, dr, mirror)
        row = lax.broadcasted_iota(jnp.int32, (TOK, TOK), 0)
        col = lax.broadcasted_iota(jnp.int32, (TOK, TOK), 1)
        ids = doc[0] if e == 0 else docs[...]
        wide = jnp.broadcast_to(ids.astype(F32), (TOK, TOK))
        allowed = (wide == wide.T) & (col <= row)
        for o in (1, 2, 3):
            arrived(KV.at[e, up(zh, -o)], kvr[e][o - 1], zfrom[o])
        kraw = jnp.concatenate([unpack(KV[e, 0]), unpack(KV[e, 1])], axis=1)
        keys = rope(kraw).astype(BF16)
        values = jnp.concatenate([unpack(KV[e, 2]), unpack(KV[e, 3])], axis=1).astype(BF16)
        gk = jnp.zeros((TOK, HEAD), F32)
        gv = jnp.zeros((TOK, HEAD), F32)
        for j in (0, 1):
            q = Qb[e, j]
            g = C[e, :, j * HEAD : (j + 1) * HEAD]
            weights = jnp.where(allowed, jnp.exp(dot(q, keys, 1, 1) * scale), 0.0)
            probs = weights / jnp.sum(weights, axis=-1, keepdims=True)
            low = probs.astype(BF16)
            att[e, :, j * HEAD : (j + 1) * HEAD] = dot(low, values, 1, 0).astype(BF16)
            gv = gv + dot(low, g, 0, 0)
            gp = dot(g, values, 1, 1)
            rdot = jnp.sum(gp * probs, axis=-1, keepdims=True)
            gs = (probs * (gp - rdot) * scale).astype(BF16)
            Gq[e, zl, xb, :, j * HEAD : (j + 1) * HEAD] = unrope(dot(gs, keys, 1, 0)).astype(BF16)
            gk = gk + dot(gs, q, 0, 0)
        gk = unrope(gk)
        for i, v in enumerate((gk[:, :64], gk[:, 64:], gv[:, :64], gv[:, 64:])):
            v = pack(v)
            gfp[e, i] = v
            gsb[e, i] = v.astype(BF16)
        for o in (1, 2, 3):
            send(gsb.at[e, up(zh, o)], grb.at[e, o - 1], gr[e][o - 1], zto[o])
        for i in range(3):
            send(Gq.at[e, zl, xb], Gq.at[e, zl, xb], xrq[e][i], square[i])
        if e == 0:
            save.append(local(att.at[0], att_out.at[0]))
        else:
            send(att.at[1], att_out.at[1], ar, mirror)

    def send_gkv(e):
        total = gfp[e, zh]
        for o in (1, 2, 3):
            arrived(grb.at[e, o - 1], gr[e][o - 1], zfrom[o])
            total = total + grb[e, o - 1].astype(F32)
        Gkvp[e, zl, xb] = total.astype(BF16)
        for i in range(3):
            send(Gkvp.at[e, zl, xb], Gkvp.at[e, zl, xb], xrk[e][i], square[i])

    def take_g(e):
        for i, (d, s) in enumerate(members):
            arrived(Gq.at[e, d, s], xrq[e][i], square[i])
            arrived(Gkvp.at[e, d, s], xrk[e][i], square[i])
        for d in (0, 1):
            Gkv[e, d] = jnp.concatenate([unpack(Gkvp[e, d, 0]), unpack(Gkvp[e, d, 1])], axis=1).astype(BF16)

    def term(e, d, zs):
        rows = features(zs)
        v = dot(Gkv[e, d], kv_weights(rows), 1, 0)
        for s in (0, 1):
            v = v + dot(Gq[e, d, s], Wq[s, rows, :], 1, 1)
        return v

    BACK = (2, 1, -1, 0)
    xs_r = [[rr.at[take("r")] for _ in BACK] for e in (0, 1)]
    zdr = [[rr.at[take("r")] for _ in (0, 1)] for e in (0, 1)]
    znr = [[rr.at[take("r")] for _ in (0, 1)] for e in (0, 1)]

    def fars(e):
        for i, k in enumerate(BACK):
            sd[e, i] = term(e, 1 - held, up(zh, k)).astype(BF16)
            send(sd.at[e, i], rd.at[e, i], xs_r[e][i], across)

    def add_half(v, other, half):
        n = TOK // 2
        other = other.astype(F32)
        if half == 0:
            return jnp.concatenate([v[:n] + other, v[n:]], axis=0)
        return jnp.concatenate([v[:n], v[n:] + other], axis=0)

    def scatter_own(e, i):
        k = BACK[i]
        v = term(e, held, up(zh, k))
        arrived(rd.at[e, i], xs_r[e][i], across)
        v = v + rd[e, i].astype(F32)
        if k == 2:
            zsd[e] = v.astype(BF16)
            for half, sign in ((0, 1), (1, -1)):
                send(zsd.at[e, HALF[half]], zrd.at[e, HALF[half]], zdr[e][half], neighbour[sign])
        elif k in (1, -1):
            half, out, into = (0, zsp, zrp) if k == 1 else (1, zsm, zrm)
            arrived(zrd.at[e, HALF[half]], zdr[e][half], neighbour[-k])
            v = add_half(v, zrd[e, HALF[half]], half)
            out[e] = v.astype(BF16)
            send(out.at[e], into.at[e], znr[e][half], neighbour[k])
        else:
            for half, sign, into in ((0, 1, zrp), (1, -1, zrm)):
                arrived(into.at[e], znr[e][half], neighbour[-sign])
                v = v + into[e].astype(F32)
            fin[e] = v.astype(BF16)

    wsr = [(rr.at[take("r")], rr.at[take("r")]) for _ in range(4)]

    def rows_out(zs, quarter):
        start = quarter * QUARTER + zs * FEAT
        return pl.ds(pl.multiple_of(start, FEAT), FEAT)

    def query_grads(zs, s):
        t = jnp.zeros((FEAT, TOK), F32)
        for e in (0, 1):
            for d in (0, 1):
                t = t + dot(X[e, d, zs], Gq[e, d, s], 0, 0)
        return t.astype(BF16)

    def weight_grads_pair(zs):
        rows = rows_out(zs, qb)
        wgq[1, zs] = query_grads(zs, 1 - xb)
        send(wgq.at[1, zs], gq_out.at[rows], wsr[zs][0], pair)
        t = jnp.zeros((HEAD, FEAT), F32)
        for e in (0, 1):
            for d in (0, 1):
                t = t + dot(Gkv[e, d], X[e, d, zs], 0, 0)
        wgkv[zs] = t.astype(BF16).reshape(2, 64, FEAT)
        send(wgkv.at[zs, 1 - xb], gkv_out.at[:, rows], wsr[zs][1], pair)
        save.append(local(wgkv.at[zs, xb], gkv_out.at[:, rows]))

    def weight_grads_own(zs):
        wgq[0, zs] = query_grads(zs, xb)
        save.append(local(wgq.at[0, zs], gq_out.at[rows_out(zs, qb)]))

    f1r = rr.at[take("r")]

    def final0(start):
        @pl.when(own)
        def _():
            keep(fin.at[0], hg_out.at[0], start)

        @pl.when(jnp.logical_not(own))
        def _():
            swap(fin.at[0], hg_out.at[0], start)

    stage0(False)
    gather_first(0)
    gather_second(0)
    gather_third(0)
    arrived(X.at[1, held, zh], s1r, swap1)
    gather_first(1)
    load_wq.wait()
    load_wkv.wait()
    arrived(Wq.at[1 - xb], wr[0], pair)
    arrived(Wkv.at[1 - xb], wr[1], pair)
    project_held(0)
    project_shared(0)
    send_partial(0)
    gather_second(1)
    send_kv(0)
    gather_third(1)
    attend(0)
    project_held(1)
    send_gkv(0)
    project_shared(1)
    send_partial(1)
    take_g(0)
    fars(0)
    send_kv(1)
    scatter_own(0, 0)
    attend(1)
    scatter_own(0, 1)
    scatter_own(0, 2)
    send_gkv(1)
    scatter_own(0, 3)
    final0(True)
    take_g(1)
    fars(1)
    for zs in range(4):
        weight_grads_pair(zs)
        scatter_own(1, zs)
    send(fin.at[1], hg_out.at[1], f1r, swap1)
    for zs in range(4):
        weight_grads_own(zs)
    final0(False)
    arrived(hg_out.at[1], f1r, swap1)
    arrived(att_out.at[1], ar, mirror)
    for zs in range(4):
        rows = rows_out(zs, 1 - qb)
        arrived(gq_out.at[rows], wsr[zs][0], pair)
        arrived(gkv_out.at[:, rows], wsr[zs][1], pair)
    for copy in save:
        copy.wait()
    for copy in pending:
        copy.wait_send()


def rope_tables():
    freqs = 10000.0 ** (-2.0 * np.arange(HEAD // 2) / HEAD)
    angles = np.arange(TOK, dtype=np.float32)[:, None] * freqs.astype(np.float32)[None, :]
    cosine, sine = np.cos(angles), np.sin(angles)
    return (
        np.concatenate([cosine, cosine], 1).astype(np.float32),
        np.concatenate([-sine, sine], 1).astype(np.float32),
    )


def body(hidden, query_weight, keyval_weight, doc_ids, cotangent):
    cosf, sinf = rope_tables()
    anywhere = pl.BlockSpec(memory_space=pl.ANY)
    vmem = pl.BlockSpec(memory_space=pltpu.VMEM)
    V = pltpu.VMEM
    big = V((2, 4, TOK, FEAT), BF16)
    mid = V((2, TOK, FEAT), BF16)
    scratch = [
        V((2, 2, 4, TOK, FEAT), BF16),
        V((2, QUARTER, 256), BF16), V((2, 64, QUARTER), BF16),
        V((2, TOK, 256), BF16), V((1, TOK), jnp.int32),
        V((2, 2, 2, TOK, 256), F32), V((2, 2, TOK, 128), F32), V((2, 2, 2, 128, 128), F32),
        V((2, 3, TOK, 256), BF16), V((2, 3, 128, 128), BF16), V((2, 3, TOK, 256), BF16), V((2, 3, 128, 128), BF16),
        V((2, 4, 128, 128), BF16),
        V((2, 4, 128, 128), F32), V((2, 4, 128, 128), BF16), V((2, 3, 128, 128), BF16),
        V((2, 2, 2, TOK, 256), BF16), V((2, 2, 2, 128, 128), BF16), V((2, 2, TOK, 128), BF16),
        V((2, 2, TOK, HEAD), BF16),
        V((2, TOK, 256), BF16),
        big, big,
        mid, mid, mid, mid, mid, mid, mid,
        V((2, 4, FEAT, 256), BF16), V((4, 2, 64, FEAT), BF16),
        pltpu.SemaphoreType.DMA((112,)),
        pltpu.SemaphoreType.DMA((96,)),
        pltpu.SemaphoreType.DMA((2, 2, 4, 2)),
        pltpu.SemaphoreType.DMA((32,)),
    ]
    att, hg, gq, gkv = pl.pallas_call(
        kernel,
        out_shape=(
            jax.ShapeDtypeStruct((2, TOK, 256), BF16),
            jax.ShapeDtypeStruct((2, TOK, FEAT), BF16),
            jax.ShapeDtypeStruct((4096, 256), BF16),
            jax.ShapeDtypeStruct((64, 4096), BF16),
        ),
        in_specs=[anywhere, anywhere, anywhere, vmem, anywhere, vmem, vmem],
        out_specs=(anywhere,) * 4,
        scratch_shapes=scratch,
        compiler_params=pltpu.CompilerParams(
            collective_id=0, has_side_effects=True, vmem_limit_bytes=60 * 2**20
        ),
    )(hidden[0], query_weight[0], keyval_weight[0].swapaxes(1, 2), doc_ids[0], cotangent[0], cosf, sinf)
    return att[None], hg[None], gq.astype(F32)[None], gkv.astype(F32).T[None]


def solution(mesh):
    sharded = P("pipe", None, "dp", "tensor")
    return jax.shard_map(
        body,
        mesh=mesh,
        in_specs=(sharded, sharded, sharded, P("pipe", None, "dp", None), sharded),
        out_specs=(sharded, sharded, P("pipe", "dp", "tensor"), P("pipe", "dp", "tensor")),
        check_vma=False,
    )
```

```python
import jax
import jax.numpy as jnp
import numpy as np
from jax import lax
from jax.experimental import pallas as pl
from jax.experimental.pallas import tpu as pltpu
from jax.sharding import PartitionSpec as P

MESH = pl.DeviceIdType.MESH
HEAD = 128
TOK = 256
FEAT = 512
F32 = jnp.float32
BF16 = jnp.bfloat16
QUARTER = 2048
PART = TOK // 2


def dot(a, b, ca, cb):
    return lax.dot_general(a, b, (((ca,), (cb,)), ((), ())), preferred_element_type=F32)


def pack(v):
    return jnp.concatenate([v[: TOK // 2], v[TOK // 2 :]], axis=1)


def unpack(v):
    v = v.astype(F32)
    return jnp.concatenate([v[:, :64], v[:, 64:]], axis=0)


def kernel(
    hid, wq, wkv, doc, cot, cosf, sinf,
    att_out, hg_out, gq_out, gkv_out,
    X, relay, Wq, Wkv, C, docs, Pq, Pkv, PkvP, sPq, sPkv, rPq, rPkv, KV, gfp, gsb, grb, Gq, Gkvp, Gkv, Qb, att,
    sd, rd, zsd, zsp, zsm, zrd, zrp, zrm, fin, wgq, wgkv,
    ss, rr, ra, ls,
):
    pipe, tens, zl = lax.axis_index("pipe"), lax.axis_index("tensor"), lax.axis_index("dp")
    x, zh = lax.div(tens, 4), lax.rem(tens, 4)
    y, c = lax.div(pipe, 2), lax.rem(pipe, 2)
    own = lax.div(x, 2) == zl

    def dev(x, y, zh, zl, c):
        return {"pipe": y * 2 + c, "tensor": x * 4 + zh, "dp": zl}

    def up(v, k):
        return lax.rem(v + k + 4, 4)

    zflip = 1 - zl
    xb = lax.rem(x, 2)
    xpair = x + 1 - 2 * xb
    held = lax.div(x, 2)
    qb = lax.rem(xb + held + zl, 2)
    neighbour = {
        1: dev(x, y, up(zh, 1), zl, c),
        -1: dev(x, y, up(zh, -1), zl, c),
        2: dev(x, y, up(zh, 2), zl, c),
    }
    across = dev(3 - x, y, zh, zl, c)
    pair = dev(xpair, y, zh, zl, c)
    square = (pair, dev(x, y, zh, zflip, c), dev(xpair, y, zh, zflip, c))
    mirror = dev(x, 3 - y, zh, zl, 1 - c)
    swap0 = dev(3 - x, y, zh, zflip, c)
    swap1 = dev(jnp.where(own, x, 3 - x), 3 - y, zh, jnp.where(own, zl, zflip), 1 - c)

    count = {"s": 0, "r": 0, "l": 0}
    pending = []
    save = []

    def take(kind):
        count[kind] += 1
        return count[kind] - 1

    def send(src, dst, rsem, to):
        copy = pltpu.make_async_remote_copy(
            src_ref=src, dst_ref=dst, send_sem=ss.at[take("s")], recv_sem=rsem, device_id=to, device_id_type=MESH
        )
        copy.start()
        pending.append(copy)

    def arrived(dst, rsem, frm):
        pltpu.make_async_remote_copy(
            src_ref=dst, dst_ref=dst, send_sem=ss.at[0], recv_sem=rsem, device_id=frm, device_id_type=MESH
        ).wait_recv()

    def local(src, dst):
        copy = pltpu.make_async_copy(src, dst, ls.at[take("l")])
        copy.start()
        return copy

    barrier = pltpu.get_barrier_semaphore()
    greet0 = dev(
        jnp.where(own, x, 3 - x), jnp.where(own, 3 - y, y), zh, jnp.where(own, zl, zflip), jnp.where(own, 1 - c, c)
    )
    for to in [neighbour[1], neighbour[-1], across, mirror, greet0] + list(square):
        pl.semaphore_signal(barrier, inc=1, device_id=to, device_id_type=MESH)
    pl.semaphore_wait(barrier, 8)

    def part(h):
        return pl.ds(h * PART, PART)

    s0s = [ss.at[take("s")] for _ in (0, 1)]
    s0r = [rr.at[take("r")] for _ in (0, 1)]
    s0l = [ls.at[take("l")] for _ in (0, 1)]

    def swap(src, dst_own, dst, h, start):
        @pl.when(own)
        def _():
            copy = pltpu.make_async_copy(src.at[part(h)], dst_own.at[part(h)], s0l[h])
            copy.start() if start else copy.wait()

        @pl.when(jnp.logical_not(own))
        def _():
            copy = pltpu.make_async_remote_copy(
                src_ref=src.at[part(h)], dst_ref=dst.at[part(h)], send_sem=s0s[h], recv_sem=s0r[h],
                device_id=swap0, device_id_type=MESH,
            )
            copy.start() if start else copy.wait()

    def stage0(h, start):
        swap(hid.at[0], X.at[0, held, zh], X.at[0, 1 - held, zh], h, start)

    s1r, cr, dr = rr.at[take("r")], rr.at[take("r")], rr.at[take("r")]
    stage0(0, True)
    stage0(1, True)
    send(hid.at[1], relay, s1r, mirror)
    s2s, s2r, s2l = ss.at[take("s")], rr.at[take("r")], ls.at[take("l")]

    def stage1(start):
        @pl.when(own)
        def _():
            copy = pltpu.make_async_copy(relay, X.at[1, held, zh], s2l)
            copy.start() if start else copy.wait()

        @pl.when(jnp.logical_not(own))
        def _():
            copy = pltpu.make_async_remote_copy(
                src_ref=relay, dst_ref=X.at[1, 1 - held, zh], send_sem=s2s, recv_sem=s2r,
                device_id=swap0, device_id_type=MESH,
            )
            copy.start() if start else copy.wait()

    mine = pl.ds(pl.multiple_of(qb * QUARTER, QUARTER), QUARTER)
    theirs = pl.ds(pl.multiple_of((1 - qb) * QUARTER, QUARTER), QUARTER)
    load_wq = local(wq.at[0, mine], Wq.at[xb])
    load_wkv = local(wkv.at[0, :, mine], Wkv.at[xb])
    wr = (rr.at[take("r")], rr.at[take("r")])
    send(wq.at[0, theirs], Wq.at[xb], wr[0], pair)
    send(wkv.at[0, :, theirs], Wkv.at[xb], wr[1], pair)
    load_c = local(cot.at[0], C.at[0])
    send(cot.at[1], C.at[1], cr, mirror)
    send(doc.at[1], docs, dr, mirror)
    Pq[...] = jnp.zeros_like(Pq)
    Pkv[...] = jnp.zeros_like(Pkv)

    def features(zs):
        return pl.ds(pl.multiple_of(zs * FEAT, FEAT), FEAT)

    def kv_weights(rows):
        return Wkv[:, :, rows].reshape(HEAD, FEAT)

    def project(e, d, zs):
        rows = features(zs)
        block = X[e, d, zs]
        for s in (0, 1):
            Pq[e, d, s] += dot(block, Wq[s, rows, :], 1, 0)
        Pkv[e, d] += dot(block, kv_weights(rows), 1, 1)

    def cut(h, half):
        if half is None:
            return part(h)
        return pl.ds(h * PART + half * (PART // 2), PART // 2)

    def slot(e, h, d, k, half):
        return X.at[e, d, up(zh, k), cut(h, half)], ra.at[e, h, d, up(zh, k), half or 0]

    def pass_on(e, h, k, half, sign):
        ref, sem = slot(e, h, held, k, half)
        send(ref, ref, sem, neighbour[sign])

    def got(e, h, k, half, sign):
        ref, sem = slot(e, h, held, k, half)
        arrived(ref, sem, neighbour[sign])

    def share(e, h, k):
        ref, sem = slot(e, h, held, k, None)
        send(ref, ref, sem, across)

    def shared(e, k):
        for h in (0, 1):
            ref, sem = slot(e, h, 1 - held, k, None)
            arrived(ref, sem, across)

    def gather_first(e, h):
        pass_on(e, h, 0, None, 1)
        pass_on(e, h, 0, None, -1)
        share(e, h, 0)

    def gather_second(e, h):
        got(e, h, -1, None, -1)
        pass_on(e, h, -1, 0, 1)
        share(e, h, -1)
        got(e, h, 1, None, 1)
        pass_on(e, h, 1, 1, -1)
        share(e, h, 1)

    def gather_third(e, h):
        got(e, h, 2, 0, -1)
        got(e, h, 2, 1, 1)
        share(e, h, 2)

    ORDER = (0, -1, 1, 2)

    def project_held(e):
        for k in ORDER:
            project(e, held, up(zh, k))

    def project_shared(e):
        for k in ORDER:
            shared(e, k)
            project(e, 1 - held, up(zh, k))

    cosw, sinw = cosf[...], sinf[...]

    def rope(v):
        return v * cosw + pltpu.roll(v, 64, 1) * sinw

    def unrope(v):
        return v * cosw - pltpu.roll(v, 64, 1) * sinw

    zto = {1: neighbour[1], 2: neighbour[2], 3: neighbour[-1]}
    zfrom = {1: neighbour[-1], 2: neighbour[2], 3: neighbour[1]}

    def three():
        return [[rr.at[take("r")] for _ in range(3)] for e in (0, 1)]

    prq, prk, kvr, gr, xrq, xrk = three(), three(), three(), three(), three(), three()
    ar = rr.at[take("r")]
    members = ((zl, 1 - xb), (zflip, xb), (zflip, 1 - xb))
    scale = HEAD**-0.5

    def send_partial(e):
        for d in (0, 1):
            for s in (0, 1):
                PkvP[e, d, s] = pack(Pkv[e, d, :, 64 * s : 64 * s + 64])
        for i, (d, s) in enumerate(members):
            sPkv[e, i] = PkvP[e, d, s].astype(BF16)
            send(sPkv.at[e, i], rPkv.at[e, i], prk[e][i], square[i])
        for i, (d, s) in enumerate(members):
            sPq[e, i] = Pq[e, d, s].astype(BF16)
            send(sPq.at[e, i], rPq.at[e, i], prq[e][i], square[i])

    def send_kv(e):
        piece = PkvP[e, zl, xb]
        for i in range(3):
            arrived(rPkv.at[e, i], prk[e][i], square[i])
            piece = piece + rPkv[e, i].astype(F32)
        KV[e, zh] = piece.astype(BF16)
        for o in (1, 2, 3):
            send(KV.at[e, zh], KV.at[e, zh], kvr[e][o - 1], zto[o])
        q = Pq[e, zl, xb]
        for i in range(3):
            arrived(rPq.at[e, i], prq[e][i], square[i])
            q = q + rPq[e, i].astype(F32)
        Qb[e, 0] = rope(q[:, :HEAD]).astype(BF16)
        Qb[e, 1] = rope(q[:, HEAD:]).astype(BF16)

    def attend(e):
        if e == 0:
            load_c.wait()
        else:
            arrived(C.at[1], cr, mirror)
            arrived(docs, dr, mirror)
        row = lax.broadcasted_iota(jnp.int32, (TOK, TOK), 0)
        col = lax.broadcasted_iota(jnp.int32, (TOK, TOK), 1)
        ids = doc[0] if e == 0 else docs[...]
        wide = jnp.broadcast_to(ids.astype(F32), (TOK, TOK))
        allowed = (wide == wide.T) & (col <= row)
        for o in (1, 2, 3):
            arrived(KV.at[e, up(zh, -o)], kvr[e][o - 1], zfrom[o])
        kraw = jnp.concatenate([unpack(KV[e, 0]), unpack(KV[e, 1])], axis=1)
        keys = rope(kraw).astype(BF16)
        values = jnp.concatenate([unpack(KV[e, 2]), unpack(KV[e, 3])], axis=1).astype(BF16)
        gk = jnp.zeros((TOK, HEAD), F32)
        gv = jnp.zeros((TOK, HEAD), F32)
        for j in (0, 1):
            q = Qb[e, j]
            g = C[e, :, j * HEAD : (j + 1) * HEAD]
            weights = jnp.where(allowed, jnp.exp(dot(q, keys, 1, 1) * scale), 0.0)
            probs = weights / jnp.sum(weights, axis=-1, keepdims=True)
            low = probs.astype(BF16)
            att[e, :, j * HEAD : (j + 1) * HEAD] = dot(low, values, 1, 0).astype(BF16)
            gv = gv + dot(low, g, 0, 0)
            gp = dot(g, values, 1, 1)
            rdot = jnp.sum(gp * probs, axis=-1, keepdims=True)
            gs = (probs * (gp - rdot) * scale).astype(BF16)
            Gq[e, zl, xb, :, j * HEAD : (j + 1) * HEAD] = unrope(dot(gs, keys, 1, 0)).astype(BF16)
            gk = gk + dot(gs, q, 0, 0)
        gk = unrope(gk)
        for i, v in enumerate((gk[:, :64], gk[:, 64:], gv[:, :64], gv[:, 64:])):
            v = pack(v)
            gfp[e, i] = v
            gsb[e, i] = v.astype(BF16)
        for o in (1, 2, 3):
            send(gsb.at[e, up(zh, o)], grb.at[e, o - 1], gr[e][o - 1], zto[o])
        for i in range(3):
            send(Gq.at[e, zl, xb], Gq.at[e, zl, xb], xrq[e][i], square[i])
        if e == 0:
            save.append(local(att.at[0], att_out.at[0]))
        else:
            send(att.at[1], att_out.at[1], ar, mirror)

    def send_gkv(e):
        total = gfp[e, zh]
        for o in (1, 2, 3):
            arrived(grb.at[e, o - 1], gr[e][o - 1], zfrom[o])
            total = total + grb[e, o - 1].astype(F32)
        Gkvp[e, zl, xb] = total.astype(BF16)
        for i in range(3):
            send(Gkvp.at[e, zl, xb], Gkvp.at[e, zl, xb], xrk[e][i], square[i])

    def take_g(e):
        for i, (d, s) in enumerate(members):
            arrived(Gq.at[e, d, s], xrq[e][i], square[i])
            arrived(Gkvp.at[e, d, s], xrk[e][i], square[i])
        for d in (0, 1):
            Gkv[e, d] = jnp.concatenate([unpack(Gkvp[e, d, 0]), unpack(Gkvp[e, d, 1])], axis=1).astype(BF16)

    def term(e, d, zs, h):
        rows = features(zs)
        v = dot(Gkv[e, d, part(h)], kv_weights(rows), 1, 0)
        for s in (0, 1):
            v = v + dot(Gq[e, d, s, part(h)], Wq[s, rows, :], 1, 1)
        return v

    BACK = (2, 1, -1, 0)

    def sems(n):
        return [[[rr.at[take("r")] for _ in range(n)] for h in (0, 1)] for e in (0, 1)]

    xs_r, zdr, znr = sems(4), sems(2), sems(2)

    def fars(e):
        for i, k in enumerate(BACK):
            for h in (0, 1):
                sd[e, i, part(h)] = term(e, 1 - held, up(zh, k), h).astype(BF16)
                send(sd.at[e, i, part(h)], rd.at[e, i, part(h)], xs_r[e][h][i], across)

    def add_half(v, other, half):
        n = PART // 2
        other = other.astype(F32)
        if half == 0:
            return jnp.concatenate([v[:n] + other, v[n:]], axis=0)
        return jnp.concatenate([v[:n], v[n:] + other], axis=0)

    def scatter_own(e, h, i):
        k, rows = BACK[i], part(h)
        v = term(e, held, up(zh, k), h)
        arrived(rd.at[e, i, rows], xs_r[e][h][i], across)
        v = v + rd[e, i, rows].astype(F32)
        if k == 2:
            zsd[e, rows] = v.astype(BF16)
            for half, sign in ((0, 1), (1, -1)):
                send(zsd.at[e, cut(h, half)], zrd.at[e, cut(h, half)], zdr[e][h][half], neighbour[sign])
        elif k in (1, -1):
            half, out, into = (0, zsp, zrp) if k == 1 else (1, zsm, zrm)
            arrived(zrd.at[e, cut(h, half)], zdr[e][h][half], neighbour[-k])
            v = add_half(v, zrd[e, cut(h, half)], half)
            out[e, rows] = v.astype(BF16)
            send(out.at[e, rows], into.at[e, rows], znr[e][h][half], neighbour[k])
        else:
            for half, sign, into in ((0, 1, zrp), (1, -1, zrm)):
                arrived(into.at[e, rows], znr[e][h][half], neighbour[-sign])
                v = v + into[e, rows].astype(F32)
            fin[e, rows] = v.astype(BF16)

    wsr = [(rr.at[take("r")], rr.at[take("r")]) for _ in range(4)]

    def rows_out(zs, quarter):
        start = quarter * QUARTER + zs * FEAT
        return pl.ds(pl.multiple_of(start, FEAT), FEAT)

    def query_grads(zs, s):
        t = jnp.zeros((FEAT, TOK), F32)
        for e in (0, 1):
            for d in (0, 1):
                t = t + dot(X[e, d, zs], Gq[e, d, s], 0, 0)
        return t.astype(BF16)

    def weight_grads_pair(zs):
        rows = rows_out(zs, qb)
        wgq[1, zs] = query_grads(zs, 1 - xb)
        send(wgq.at[1, zs], gq_out.at[rows], wsr[zs][0], pair)
        t = jnp.zeros((HEAD, FEAT), F32)
        for e in (0, 1):
            for d in (0, 1):
                t = t + dot(Gkv[e, d], X[e, d, zs], 0, 0)
        wgkv[zs] = t.astype(BF16).reshape(2, 64, FEAT)
        send(wgkv.at[zs, 1 - xb], gkv_out.at[:, rows], wsr[zs][1], pair)
        save.append(local(wgkv.at[zs, xb], gkv_out.at[:, rows]))

    def weight_grads_own(zs):
        wgq[0, zs] = query_grads(zs, xb)
        save.append(local(wgq.at[0, zs], gq_out.at[rows_out(zs, qb)]))

    f1r = [rr.at[take("r")] for _ in (0, 1)]

    def final0(h, start):
        swap(fin.at[0], hg_out.at[0], hg_out.at[0], h, start)

    for h in (0, 1):
        stage0(h, False)
        gather_first(0, h)
    arrived(relay, s1r, mirror)
    stage1(True)
    gather_second(0, 0)
    gather_second(0, 1)
    gather_third(0, 0)
    gather_third(0, 1)
    stage1(False)
    gather_first(1, 0)
    gather_first(1, 1)
    load_wq.wait()
    load_wkv.wait()
    arrived(Wq.at[1 - xb], wr[0], pair)
    arrived(Wkv.at[1 - xb], wr[1], pair)
    project_held(0)
    for k in (0, -1):
        shared(0, k)
        project(0, 1 - held, up(zh, k))
    gather_second(1, 0)
    gather_second(1, 1)
    for k in (1, 2):
        shared(0, k)
        project(0, 1 - held, up(zh, k))
    send_partial(0)
    gather_third(1, 0)
    gather_third(1, 1)
    send_kv(0)
    attend(0)
    project_held(1)
    send_gkv(0)
    project_shared(1)
    send_partial(1)
    take_g(0)
    fars(0)
    send_kv(1)
    scatter_own(0, 0, 0)
    scatter_own(0, 1, 0)
    attend(1)
    scatter_own(0, 0, 1)
    scatter_own(0, 1, 1)
    send_gkv(1)
    scatter_own(0, 0, 2)
    scatter_own(0, 1, 2)
    take_g(1)
    fars(1)
    for h in (0, 1):
        scatter_own(0, h, 3)
        final0(h, True)
    weight_grads_pair(0)
    weight_grads_pair(1)
    scatter_own(1, 0, 0)
    scatter_own(1, 1, 0)
    weight_grads_pair(2)
    weight_grads_pair(3)
    for i in (1, 2):
        for h in (0, 1):
            scatter_own(1, h, i)
    weight_grads_own(0)
    weight_grads_own(1)
    for h in (0, 1):
        scatter_own(1, h, 3)
        send(fin.at[1, part(h)], hg_out.at[1, part(h)], f1r[h], swap1)
    weight_grads_own(2)
    weight_grads_own(3)
    for h in (0, 1):
        final0(h, False)
        arrived(hg_out.at[1, part(h)], f1r[h], swap1)
    arrived(att_out.at[1], ar, mirror)
    for zs in range(4):
        rows = rows_out(zs, 1 - qb)
        arrived(gq_out.at[rows], wsr[zs][0], pair)
        arrived(gkv_out.at[:, rows], wsr[zs][1], pair)
    for copy in save:
        copy.wait()
    for copy in pending:
        copy.wait_send()


def finish(att, hg, gq, gkv, att_out, hg_out, gq_out, gkv_out):
    att_out[...] = att[...]
    hg_out[...] = hg[...]
    gq_out[...] = gq[...].astype(F32)
    gkv_out[...] = gkv[...].astype(F32)


def rope_tables():
    freqs = 10000.0 ** (-2.0 * np.arange(HEAD // 2) / HEAD)
    angles = np.arange(TOK, dtype=np.float32)[:, None] * freqs.astype(np.float32)[None, :]
    cosine, sine = np.cos(angles), np.sin(angles)
    return (
        np.concatenate([cosine, cosine], 1).astype(np.float32),
        np.concatenate([-sine, sine], 1).astype(np.float32),
    )


def body(hidden, query_weight, keyval_weight, doc_ids, cotangent):
    cosf, sinf = rope_tables()
    anywhere = pl.BlockSpec(memory_space=pl.ANY)
    vmem = pl.BlockSpec(memory_space=pltpu.VMEM)
    V = pltpu.VMEM
    big = V((2, 4, TOK, FEAT), BF16)
    mid = V((2, TOK, FEAT), BF16)
    scratch = [
        V((2, 2, 4, TOK, FEAT), BF16), V((TOK, FEAT), BF16),
        V((2, QUARTER, 256), BF16), V((2, 64, QUARTER), BF16),
        V((2, TOK, 256), BF16), V((1, TOK), jnp.int32),
        V((2, 2, 2, TOK, 256), F32), V((2, 2, TOK, 128), F32), V((2, 2, 2, 128, 128), F32),
        V((2, 3, TOK, 256), BF16), V((2, 3, 128, 128), BF16), V((2, 3, TOK, 256), BF16), V((2, 3, 128, 128), BF16),
        V((2, 4, 128, 128), BF16),
        V((2, 4, 128, 128), F32), V((2, 4, 128, 128), BF16), V((2, 3, 128, 128), BF16),
        V((2, 2, 2, TOK, 256), BF16), V((2, 2, 2, 128, 128), BF16), V((2, 2, TOK, 128), BF16),
        V((2, 2, TOK, HEAD), BF16),
        V((2, TOK, 256), BF16),
        big, big,
        mid, mid, mid, mid, mid, mid, mid,
        V((2, 4, FEAT, 256), BF16), V((4, 2, 64, FEAT), BF16),
        pltpu.SemaphoreType.DMA((160,)),
        pltpu.SemaphoreType.DMA((128,)),
        pltpu.SemaphoreType.DMA((2, 2, 2, 4, 2)),
        pltpu.SemaphoreType.DMA((32,)),
    ]
    att, hg, gq, gkv = pl.pallas_call(
        kernel,
        out_shape=(
            jax.ShapeDtypeStruct((2, TOK, 256), BF16),
            jax.ShapeDtypeStruct((2, TOK, FEAT), BF16),
            jax.ShapeDtypeStruct((4096, 256), BF16),
            jax.ShapeDtypeStruct((64, 4096), BF16),
        ),
        in_specs=[anywhere, anywhere, anywhere, vmem, anywhere, vmem, vmem],
        out_specs=(anywhere,) * 4,
        scratch_shapes=scratch,
        compiler_params=pltpu.CompilerParams(
            collective_id=0, has_side_effects=True, vmem_limit_bytes=60 * 2**20
        ),
    )(hidden[0], query_weight[0], keyval_weight[0].swapaxes(1, 2), doc_ids[0], cotangent[0], cosf, sinf)
    steps = 4
    specs = (
        pl.BlockSpec((2, TOK // steps, 256), lambda i: (0, i, 0)),
        pl.BlockSpec((2, TOK // steps, FEAT), lambda i: (0, i, 0)),
        pl.BlockSpec((4096 // steps, 256), lambda i: (i, 0)),
        pl.BlockSpec((64, 4096 // steps), lambda i: (0, i)),
    )
    att, hg, gq, gkv = pl.pallas_call(
        finish,
        grid=(steps,),
        out_shape=(
            jax.ShapeDtypeStruct(att.shape, BF16),
            jax.ShapeDtypeStruct(hg.shape, BF16),
            jax.ShapeDtypeStruct(gq.shape, F32),
            jax.ShapeDtypeStruct(gkv.shape, F32),
        ),
        in_specs=list(specs),
        out_specs=specs,
        compiler_params=pltpu.CompilerParams(vmem_limit_bytes=60 * 2**20),
    )(att, hg, gq, gkv)
    return att[None], hg[None], gq[None], gkv.T[None]


def solution(mesh):
    sharded = P("pipe", None, "dp", "tensor")
    return jax.shard_map(
        body,
        mesh=mesh,
        in_specs=(sharded, sharded, sharded, P("pipe", None, "dp", None), sharded),
        out_specs=(sharded, sharded, P("pipe", "dp", "tensor"), P("pipe", "dp", "tensor")),
        check_vma=False,
    )
```

```python
import jax
import jax.numpy as jnp
import numpy as np
from jax import lax
from jax.experimental import pallas as pl
from jax.experimental.pallas import tpu as pltpu
from jax.sharding import PartitionSpec as P

MESH = pl.DeviceIdType.MESH
HEAD = 128
TOK = 256
FEAT = 512
F32 = jnp.float32
BF16 = jnp.bfloat16
QUARTER = 2048
PART = TOK // 2


def dot(a, b, ca, cb):
    return lax.dot_general(a, b, (((ca,), (cb,)), ((), ())), preferred_element_type=F32)


def pack(v):
    return jnp.concatenate([v[: TOK // 2], v[TOK // 2 :]], axis=1)


def unpack(v):
    v = v.astype(F32)
    return jnp.concatenate([v[:, :64], v[:, 64:]], axis=0)


def kernel(
    hid, wq, wkv, doc, cot, cosf, sinf,
    att_out, hg_out, gq_out, gkv_out,
    X, relay, Wq, Wkv, C, docs, Pq, Pkv, PkvP, sPq, sPkv, rPq, rPkv, KV, gfp, gsb, grb, Gq, Gkvp, Gkv, Qb, att,
    sd, rd, zsd, zsp, zsm, zrd, zrp, zrm, fin, wgq, wgkv,
    ss, rr, ra, ls,
):
    pipe, tens, zl = lax.axis_index("pipe"), lax.axis_index("tensor"), lax.axis_index("dp")
    x, zh = lax.div(tens, 4), lax.rem(tens, 4)
    y, c = lax.div(pipe, 2), lax.rem(pipe, 2)
    own = lax.div(x, 2) == zl

    def dev(x, y, zh, zl, c):
        return {"pipe": y * 2 + c, "tensor": x * 4 + zh, "dp": zl}

    def up(v, k):
        return lax.rem(v + k + 4, 4)

    zflip = 1 - zl
    xb = lax.rem(x, 2)
    xpair = x + 1 - 2 * xb
    held = lax.div(x, 2)
    qb = lax.rem(xb + held + zl, 2)
    neighbour = {
        1: dev(x, y, up(zh, 1), zl, c),
        -1: dev(x, y, up(zh, -1), zl, c),
        2: dev(x, y, up(zh, 2), zl, c),
    }
    across = dev(3 - x, y, zh, zl, c)
    pair = dev(xpair, y, zh, zl, c)
    square = (pair, dev(x, y, zh, zflip, c), dev(xpair, y, zh, zflip, c))
    mirror = dev(x, 3 - y, zh, zl, 1 - c)
    swap0 = dev(3 - x, y, zh, zflip, c)
    swap1 = dev(jnp.where(own, x, 3 - x), 3 - y, zh, jnp.where(own, zl, zflip), 1 - c)

    count = {"s": 0, "r": 0, "l": 0}
    pending = []
    save = []

    def take(kind):
        count[kind] += 1
        return count[kind] - 1

    def send(src, dst, rsem, to):
        copy = pltpu.make_async_remote_copy(
            src_ref=src, dst_ref=dst, send_sem=ss.at[take("s")], recv_sem=rsem, device_id=to, device_id_type=MESH
        )
        copy.start()
        pending.append(copy)

    def arrived(dst, rsem, frm):
        pltpu.make_async_remote_copy(
            src_ref=dst, dst_ref=dst, send_sem=ss.at[0], recv_sem=rsem, device_id=frm, device_id_type=MESH
        ).wait_recv()

    def local(src, dst):
        copy = pltpu.make_async_copy(src, dst, ls.at[take("l")])
        copy.start()
        return copy

    barrier = pltpu.get_barrier_semaphore()
    greet0 = dev(
        jnp.where(own, x, 3 - x), jnp.where(own, 3 - y, y), zh, jnp.where(own, zl, zflip), jnp.where(own, 1 - c, c)
    )
    for to in [neighbour[1], neighbour[-1], across, mirror, greet0] + list(square):
        pl.semaphore_signal(barrier, inc=1, device_id=to, device_id_type=MESH)
    pl.semaphore_wait(barrier, 8)

    def part(h):
        return pl.ds(h * PART, PART)

    s0s = [ss.at[take("s")] for _ in (0, 1)]
    s0r = [rr.at[take("r")] for _ in (0, 1)]
    s0l = [ls.at[take("l")] for _ in (0, 1)]

    def swap(src, dst_own, dst, h, start):
        @pl.when(own)
        def _():
            copy = pltpu.make_async_copy(src.at[part(h)], dst_own.at[part(h)], s0l[h])
            copy.start() if start else copy.wait()

        @pl.when(jnp.logical_not(own))
        def _():
            copy = pltpu.make_async_remote_copy(
                src_ref=src.at[part(h)], dst_ref=dst.at[part(h)], send_sem=s0s[h], recv_sem=s0r[h],
                device_id=swap0, device_id_type=MESH,
            )
            copy.start() if start else copy.wait()

    def stage0(h, start):
        swap(hid.at[0], X.at[0, held, zh], X.at[0, 1 - held, zh], h, start)

    s1r, cr, dr = rr.at[take("r")], rr.at[take("r")], rr.at[take("r")]
    stage0(0, True)
    stage0(1, True)
    send(hid.at[1], relay, s1r, mirror)
    s2s, s2r, s2l = ss.at[take("s")], rr.at[take("r")], ls.at[take("l")]

    def stage1(start):
        @pl.when(own)
        def _():
            copy = pltpu.make_async_copy(relay, X.at[1, held, zh], s2l)
            copy.start() if start else copy.wait()

        @pl.when(jnp.logical_not(own))
        def _():
            copy = pltpu.make_async_remote_copy(
                src_ref=relay, dst_ref=X.at[1, 1 - held, zh], send_sem=s2s, recv_sem=s2r,
                device_id=swap0, device_id_type=MESH,
            )
            copy.start() if start else copy.wait()

    mine = pl.ds(pl.multiple_of(qb * QUARTER, QUARTER), QUARTER)
    theirs = pl.ds(pl.multiple_of((1 - qb) * QUARTER, QUARTER), QUARTER)
    load_wq = local(wq.at[0, mine], Wq.at[xb])
    load_wkv = local(wkv.at[0, :, mine], Wkv.at[xb])
    wr = (rr.at[take("r")], rr.at[take("r")])
    send(wq.at[0, theirs], Wq.at[xb], wr[0], pair)
    send(wkv.at[0, :, theirs], Wkv.at[xb], wr[1], pair)
    load_c = local(cot.at[0], C.at[0])
    send(cot.at[1], C.at[1], cr, mirror)
    send(doc.at[1], docs, dr, mirror)
    Pq[...] = jnp.zeros_like(Pq)
    Pkv[...] = jnp.zeros_like(Pkv)

    def features(zs):
        return pl.ds(pl.multiple_of(zs * FEAT, FEAT), FEAT)

    def kv_weights(rows):
        return Wkv[:, :, rows].reshape(HEAD, FEAT)

    def project(e, d, zs):
        rows = features(zs)
        block = X[e, d, zs]
        for s in (0, 1):
            Pq[e, d, s] += dot(block, Wq[s, rows, :], 1, 0)
        Pkv[e, d] += dot(block, kv_weights(rows), 1, 1)

    def cut(h, half):
        if half is None:
            return part(h)
        return pl.ds(h * PART + half * (PART // 2), PART // 2)

    def slot(e, h, d, k, half):
        return X.at[e, d, up(zh, k), cut(h, half)], ra.at[e, h, d, up(zh, k), half or 0]

    def pass_on(e, h, k, half, sign):
        ref, sem = slot(e, h, held, k, half)
        send(ref, ref, sem, neighbour[sign])

    def got(e, h, k, half, sign):
        ref, sem = slot(e, h, held, k, half)
        arrived(ref, sem, neighbour[sign])

    def share(e, h, k):
        ref, sem = slot(e, h, held, k, None)
        send(ref, ref, sem, across)

    def shared(e, k):
        for h in (0, 1):
            ref, sem = slot(e, h, 1 - held, k, None)
            arrived(ref, sem, across)

    def gather_first(e, h):
        pass_on(e, h, 0, None, 1)
        pass_on(e, h, 0, None, -1)
        share(e, h, 0)

    def gather_second(e, h):
        got(e, h, -1, None, -1)
        pass_on(e, h, -1, 0, 1)
        share(e, h, -1)
        got(e, h, 1, None, 1)
        pass_on(e, h, 1, 1, -1)
        share(e, h, 1)

    def gather_third(e, h):
        got(e, h, 2, 0, -1)
        got(e, h, 2, 1, 1)
        share(e, h, 2)

    ORDER = (0, -1, 1, 2)

    def project_held(e):
        for k in ORDER:
            project(e, held, up(zh, k))

    def project_shared(e):
        for k in ORDER:
            shared(e, k)
            project(e, 1 - held, up(zh, k))

    cosw, sinw = cosf[...], sinf[...]

    def rope(v):
        return v * cosw + pltpu.roll(v, 64, 1) * sinw

    def unrope(v):
        return v * cosw - pltpu.roll(v, 64, 1) * sinw

    zto = {1: neighbour[1], 2: neighbour[2], 3: neighbour[-1]}
    zfrom = {1: neighbour[-1], 2: neighbour[2], 3: neighbour[1]}

    def three():
        return [[rr.at[take("r")] for _ in range(3)] for e in (0, 1)]

    prq, prk, kvr, gr, xrq, xrk = three(), three(), three(), three(), three(), three()
    ar = rr.at[take("r")]
    members = ((zl, 1 - xb), (zflip, xb), (zflip, 1 - xb))
    scale = HEAD**-0.5

    def send_partial(e):
        for d in (0, 1):
            for s in (0, 1):
                PkvP[e, d, s] = pack(Pkv[e, d, :, 64 * s : 64 * s + 64])
        for i, (d, s) in enumerate(members):
            sPkv[e, i] = PkvP[e, d, s].astype(BF16)
            send(sPkv.at[e, i], rPkv.at[e, i], prk[e][i], square[i])
        for i, (d, s) in enumerate(members):
            sPq[e, i] = Pq[e, d, s].astype(BF16)
            send(sPq.at[e, i], rPq.at[e, i], prq[e][i], square[i])

    def send_kv(e):
        piece = PkvP[e, zl, xb]
        for i in range(3):
            arrived(rPkv.at[e, i], prk[e][i], square[i])
            piece = piece + rPkv[e, i].astype(F32)
        KV[e, zh] = piece.astype(BF16)
        for o in (1, 2, 3):
            send(KV.at[e, zh], KV.at[e, zh], kvr[e][o - 1], zto[o])
        q = Pq[e, zl, xb]
        for i in range(3):
            arrived(rPq.at[e, i], prq[e][i], square[i])
            q = q + rPq[e, i].astype(F32)
        Qb[e, 0] = rope(q[:, :HEAD]).astype(BF16)
        Qb[e, 1] = rope(q[:, HEAD:]).astype(BF16)

    def attend(e):
        if e == 0:
            load_c.wait()
        else:
            arrived(C.at[1], cr, mirror)
            arrived(docs, dr, mirror)
        row = lax.broadcasted_iota(jnp.int32, (TOK, TOK), 0)
        col = lax.broadcasted_iota(jnp.int32, (TOK, TOK), 1)
        ids = doc[0] if e == 0 else docs[...]
        wide = jnp.broadcast_to(ids.astype(F32), (TOK, TOK))
        allowed = (wide == wide.T) & (col <= row)
        for o in (1, 2, 3):
            arrived(KV.at[e, up(zh, -o)], kvr[e][o - 1], zfrom[o])
        kraw = jnp.concatenate([unpack(KV[e, 0]), unpack(KV[e, 1])], axis=1)
        keys = rope(kraw).astype(BF16)
        values = jnp.concatenate([unpack(KV[e, 2]), unpack(KV[e, 3])], axis=1).astype(BF16)
        gk = jnp.zeros((TOK, HEAD), F32)
        gv = jnp.zeros((TOK, HEAD), F32)
        for j in (0, 1):
            q = Qb[e, j]
            g = C[e, :, j * HEAD : (j + 1) * HEAD]
            weights = jnp.where(allowed, jnp.exp(dot(q, keys, 1, 1) * scale), 0.0)
            probs = weights / jnp.sum(weights, axis=-1, keepdims=True)
            low = probs.astype(BF16)
            att[e, :, j * HEAD : (j + 1) * HEAD] = dot(low, values, 1, 0).astype(BF16)
            gv = gv + dot(low, g, 0, 0)
            gp = dot(g, values, 1, 1)
            rdot = jnp.sum(gp * probs, axis=-1, keepdims=True)
            gs = (probs * (gp - rdot) * scale).astype(BF16)
            Gq[e, zl, xb, :, j * HEAD : (j + 1) * HEAD] = unrope(dot(gs, keys, 1, 0)).astype(BF16)
            gk = gk + dot(gs, q, 0, 0)
        gk = unrope(gk)
        for i, v in enumerate((gk[:, :64], gk[:, 64:], gv[:, :64], gv[:, 64:])):
            v = pack(v)
            gfp[e, i] = v
            gsb[e, i] = v.astype(BF16)
        for o in (1, 2, 3):
            send(gsb.at[e, up(zh, o)], grb.at[e, o - 1], gr[e][o - 1], zto[o])
        for i in range(3):
            send(Gq.at[e, zl, xb], Gq.at[e, zl, xb], xrq[e][i], square[i])
        if e == 0:
            save.append(local(att.at[0], att_out.at[0]))
        else:
            send(att.at[1], att_out.at[1], ar, mirror)

    def send_gkv(e):
        total = gfp[e, zh]
        for o in (1, 2, 3):
            arrived(grb.at[e, o - 1], gr[e][o - 1], zfrom[o])
            total = total + grb[e, o - 1].astype(F32)
        Gkvp[e, zl, xb] = total.astype(BF16)
        for i in range(3):
            send(Gkvp.at[e, zl, xb], Gkvp.at[e, zl, xb], xrk[e][i], square[i])

    def take_g(e):
        for i, (d, s) in enumerate(members):
            arrived(Gq.at[e, d, s], xrq[e][i], square[i])
            arrived(Gkvp.at[e, d, s], xrk[e][i], square[i])
        for d in (0, 1):
            Gkv[e, d] = jnp.concatenate([unpack(Gkvp[e, d, 0]), unpack(Gkvp[e, d, 1])], axis=1).astype(BF16)

    def term(e, d, zs, h):
        rows = features(zs)
        v = dot(Gkv[e, d, part(h)], kv_weights(rows), 1, 0)
        for s in (0, 1):
            v = v + dot(Gq[e, d, s, part(h)], Wq[s, rows, :], 1, 1)
        return v

    BACK = (2, 1, -1, 0)

    def sems(n):
        return [[[rr.at[take("r")] for _ in range(n)] for h in (0, 1)] for e in (0, 1)]

    xs_r, zdr, znr = sems(4), sems(2), sems(2)

    def fars(e):
        for i, k in enumerate(BACK):
            for h in (0, 1):
                sd[e, i, part(h)] = term(e, 1 - held, up(zh, k), h).astype(BF16)
                send(sd.at[e, i, part(h)], rd.at[e, i, part(h)], xs_r[e][h][i], across)

    def add_half(v, other, half):
        n = PART // 2
        other = other.astype(F32)
        if half == 0:
            return jnp.concatenate([v[:n] + other, v[n:]], axis=0)
        return jnp.concatenate([v[:n], v[n:] + other], axis=0)

    def scatter_own(e, h, i):
        k, rows = BACK[i], part(h)
        v = term(e, held, up(zh, k), h)
        arrived(rd.at[e, i, rows], xs_r[e][h][i], across)
        v = v + rd[e, i, rows].astype(F32)
        if k == 2:
            zsd[e, rows] = v.astype(BF16)
            for half, sign in ((0, 1), (1, -1)):
                send(zsd.at[e, cut(h, half)], zrd.at[e, cut(h, half)], zdr[e][h][half], neighbour[sign])
        elif k in (1, -1):
            half, out, into = (0, zsp, zrp) if k == 1 else (1, zsm, zrm)
            arrived(zrd.at[e, cut(h, half)], zdr[e][h][half], neighbour[-k])
            v = add_half(v, zrd[e, cut(h, half)], half)
            out[e, rows] = v.astype(BF16)
            send(out.at[e, rows], into.at[e, rows], znr[e][h][half], neighbour[k])
        else:
            for half, sign, into in ((0, 1, zrp), (1, -1, zrm)):
                arrived(into.at[e, rows], znr[e][h][half], neighbour[-sign])
                v = v + into[e, rows].astype(F32)
            fin[e, rows] = v.astype(BF16)

    wsr = [(rr.at[take("r")], rr.at[take("r")]) for _ in range(4)]

    def rows_out(zs, quarter):
        start = quarter * QUARTER + zs * FEAT
        return pl.ds(pl.multiple_of(start, FEAT), FEAT)

    def query_grads(zs, s):
        t = jnp.zeros((FEAT, TOK), F32)
        for e in (0, 1):
            for d in (0, 1):
                t = t + dot(X[e, d, zs], Gq[e, d, s], 0, 0)
        return t.astype(BF16)

    def weight_grads_pair(zs):
        rows = rows_out(zs, qb)
        wgq[1, zs] = query_grads(zs, 1 - xb)
        send(wgq.at[1, zs], gq_out.at[rows], wsr[zs][0], pair)
        t = jnp.zeros((HEAD, FEAT), F32)
        for e in (0, 1):
            for d in (0, 1):
                t = t + dot(Gkv[e, d], X[e, d, zs], 0, 0)
        wgkv[zs] = t.astype(BF16).reshape(2, 64, FEAT)
        send(wgkv.at[zs, 1 - xb], gkv_out.at[:, rows], wsr[zs][1], pair)
        save.append(local(wgkv.at[zs, xb], gkv_out.at[:, rows]))

    def weight_grads_own(zs):
        wgq[0, zs] = query_grads(zs, xb)
        save.append(local(wgq.at[0, zs], gq_out.at[rows_out(zs, qb)]))

    f1r = [rr.at[take("r")] for _ in (0, 1)]

    def final0(h, start):
        swap(fin.at[0], hg_out.at[0], hg_out.at[0], h, start)

    for h in (0, 1):
        stage0(h, False)
        gather_first(0, h)
    arrived(relay, s1r, mirror)
    stage1(True)
    gather_second(0, 0)
    gather_second(0, 1)
    stage1(False)
    gather_first(1, 0)
    gather_first(1, 1)
    gather_third(0, 0)
    gather_third(0, 1)
    load_wq.wait()
    load_wkv.wait()
    arrived(Wq.at[1 - xb], wr[0], pair)
    arrived(Wkv.at[1 - xb], wr[1], pair)
    project_held(0)
    gather_second(1, 0)
    gather_second(1, 1)
    for k in ORDER:
        shared(0, k)
        project(0, 1 - held, up(zh, k))
    send_partial(0)
    gather_third(1, 0)
    gather_third(1, 1)
    send_kv(0)
    attend(0)
    project_held(1)
    send_gkv(0)
    project_shared(1)
    send_partial(1)
    take_g(0)
    fars(0)
    send_kv(1)
    scatter_own(0, 0, 0)
    scatter_own(0, 1, 0)
    attend(1)
    scatter_own(0, 0, 1)
    scatter_own(0, 1, 1)
    send_gkv(1)
    scatter_own(0, 0, 2)
    scatter_own(0, 1, 2)
    take_g(1)
    fars(1)
    for h in (0, 1):
        scatter_own(0, h, 3)
        final0(h, True)
    weight_grads_pair(0)
    weight_grads_pair(1)
    scatter_own(1, 0, 0)
    scatter_own(1, 1, 0)
    weight_grads_pair(2)
    weight_grads_pair(3)
    for i in (1, 2):
        for h in (0, 1):
            scatter_own(1, h, i)
    weight_grads_own(0)
    weight_grads_own(1)
    for h in (0, 1):
        scatter_own(1, h, 3)
        send(fin.at[1, part(h)], hg_out.at[1, part(h)], f1r[h], swap1)
    weight_grads_own(2)
    weight_grads_own(3)
    for h in (0, 1):
        final0(h, False)
        arrived(hg_out.at[1, part(h)], f1r[h], swap1)
    arrived(att_out.at[1], ar, mirror)
    for zs in range(4):
        rows = rows_out(zs, 1 - qb)
        arrived(gq_out.at[rows], wsr[zs][0], pair)
        arrived(gkv_out.at[:, rows], wsr[zs][1], pair)
    for copy in save:
        copy.wait()
    for copy in pending:
        copy.wait_send()


def finish(att, hg, gq, gkv, att_out, hg_out, gq_out, gkv_out):
    att_out[...] = att[...]
    hg_out[...] = hg[...]
    gq_out[...] = gq[...].astype(F32)
    gkv_out[...] = gkv[...].astype(F32)


def rope_tables():
    freqs = 10000.0 ** (-2.0 * np.arange(HEAD // 2) / HEAD)
    angles = np.arange(TOK, dtype=np.float32)[:, None] * freqs.astype(np.float32)[None, :]
    cosine, sine = np.cos(angles), np.sin(angles)
    return (
        np.concatenate([cosine, cosine], 1).astype(np.float32),
        np.concatenate([-sine, sine], 1).astype(np.float32),
    )


def body(hidden, query_weight, keyval_weight, doc_ids, cotangent):
    cosf, sinf = rope_tables()
    anywhere = pl.BlockSpec(memory_space=pl.ANY)
    vmem = pl.BlockSpec(memory_space=pltpu.VMEM)
    V = pltpu.VMEM
    big = V((2, 4, TOK, FEAT), BF16)
    mid = V((2, TOK, FEAT), BF16)
    scratch = [
        V((2, 2, 4, TOK, FEAT), BF16), V((TOK, FEAT), BF16),
        V((2, QUARTER, 256), BF16), V((2, 64, QUARTER), BF16),
        V((2, TOK, 256), BF16), V((1, TOK), jnp.int32),
        V((2, 2, 2, TOK, 256), F32), V((2, 2, TOK, 128), F32), V((2, 2, 2, 128, 128), F32),
        V((2, 3, TOK, 256), BF16), V((2, 3, 128, 128), BF16), V((2, 3, TOK, 256), BF16), V((2, 3, 128, 128), BF16),
        V((2, 4, 128, 128), BF16),
        V((2, 4, 128, 128), F32), V((2, 4, 128, 128), BF16), V((2, 3, 128, 128), BF16),
        V((2, 2, 2, TOK, 256), BF16), V((2, 2, 2, 128, 128), BF16), V((2, 2, TOK, 128), BF16),
        V((2, 2, TOK, HEAD), BF16),
        V((2, TOK, 256), BF16),
        big, big,
        mid, mid, mid, mid, mid, mid, mid,
        V((2, 4, FEAT, 256), BF16), V((4, 2, 64, FEAT), BF16),
        pltpu.SemaphoreType.DMA((160,)),
        pltpu.SemaphoreType.DMA((128,)),
        pltpu.SemaphoreType.DMA((2, 2, 2, 4, 2)),
        pltpu.SemaphoreType.DMA((32,)),
    ]
    att, hg, gq, gkv = pl.pallas_call(
        kernel,
        out_shape=(
            jax.ShapeDtypeStruct((2, TOK, 256), BF16),
            jax.ShapeDtypeStruct((2, TOK, FEAT), BF16),
            jax.ShapeDtypeStruct((4096, 256), BF16),
            jax.ShapeDtypeStruct((64, 4096), BF16),
        ),
        in_specs=[anywhere, anywhere, anywhere, vmem, anywhere, vmem, vmem],
        out_specs=(anywhere,) * 4,
        scratch_shapes=scratch,
        compiler_params=pltpu.CompilerParams(
            collective_id=0, has_side_effects=True, vmem_limit_bytes=60 * 2**20
        ),
    )(hidden[0], query_weight[0], keyval_weight[0].swapaxes(1, 2), doc_ids[0], cotangent[0], cosf, sinf)
    steps = 4
    specs = (
        pl.BlockSpec((2, TOK // steps, 256), lambda i: (0, i, 0)),
        pl.BlockSpec((2, TOK // steps, FEAT), lambda i: (0, i, 0)),
        pl.BlockSpec((4096 // steps, 256), lambda i: (i, 0)),
        pl.BlockSpec((64, 4096 // steps), lambda i: (0, i)),
    )
    att, hg, gq, gkv = pl.pallas_call(
        finish,
        grid=(steps,),
        out_shape=(
            jax.ShapeDtypeStruct(att.shape, BF16),
            jax.ShapeDtypeStruct(hg.shape, BF16),
            jax.ShapeDtypeStruct(gq.shape, F32),
            jax.ShapeDtypeStruct(gkv.shape, F32),
        ),
        in_specs=list(specs),
        out_specs=specs,
        compiler_params=pltpu.CompilerParams(vmem_limit_bytes=60 * 2**20),
    )(att, hg, gq, gkv)
    return att[None], hg[None], gq[None], gkv.T[None]


def solution(mesh):
    sharded = P("pipe", None, "dp", "tensor")
    return jax.shard_map(
        body,
        mesh=mesh,
        in_specs=(sharded, sharded, sharded, P("pipe", None, "dp", None), sharded),
        out_specs=(sharded, sharded, P("pipe", "dp", "tensor"), P("pipe", "dp", "tensor")),
        check_vma=False,
    )
```

```python
import jax
import jax.numpy as jnp
import numpy as np
from jax import lax
from jax.experimental import pallas as pl
from jax.experimental.pallas import tpu as pltpu
from jax.sharding import PartitionSpec as P

MESH = pl.DeviceIdType.MESH
HEAD = 128
TOK = 256
FEAT = 512
F32 = jnp.float32
BF16 = jnp.bfloat16
QUARTER = 2048
PART = TOK // 2


def dot(a, b, ca, cb):
    return lax.dot_general(a, b, (((ca,), (cb,)), ((), ())), preferred_element_type=F32)


def pack(v):
    return jnp.concatenate([v[: TOK // 2], v[TOK // 2 :]], axis=1)


def unpack(v):
    v = v.astype(F32)
    return jnp.concatenate([v[:, :64], v[:, 64:]], axis=0)


def kernel(
    hid, wq, wkv, doc, cot, cosf, sinf,
    att_out, hg_out, gq_out, gkv_out,
    X, relay, Wq, Wkv, C, docs, Pq, Pkv, PkvP, sPq, sPkv, rPq, rPkv, KV, gfp, gsb, grb, Gq, Gkvp, Gkv, Qb, att,
    sd, rd, zsd, zsp, zsm, zrd, zrp, zrm, fin, wgq, wgkv,
    ss, rr, ra, ls,
):
    pipe, tens, zl = lax.axis_index("pipe"), lax.axis_index("tensor"), lax.axis_index("dp")
    x, zh = lax.div(tens, 4), lax.rem(tens, 4)
    y, c = lax.div(pipe, 2), lax.rem(pipe, 2)
    own = lax.div(x, 2) == zl

    def dev(x, y, zh, zl, c):
        return {"pipe": y * 2 + c, "tensor": x * 4 + zh, "dp": zl}

    def up(v, k):
        return lax.rem(v + k + 4, 4)

    zflip = 1 - zl
    xb = lax.rem(x, 2)
    xpair = x + 1 - 2 * xb
    held = lax.div(x, 2)
    qb = lax.rem(xb + held + zl, 2)
    neighbour = {
        1: dev(x, y, up(zh, 1), zl, c),
        -1: dev(x, y, up(zh, -1), zl, c),
        2: dev(x, y, up(zh, 2), zl, c),
    }
    across = dev(3 - x, y, zh, zl, c)
    pair = dev(xpair, y, zh, zl, c)
    square = (pair, dev(x, y, zh, zflip, c), dev(xpair, y, zh, zflip, c))
    mirror = dev(x, 3 - y, zh, zl, 1 - c)
    swap0 = dev(3 - x, y, zh, zflip, c)
    swap1 = dev(jnp.where(own, x, 3 - x), 3 - y, zh, jnp.where(own, zl, zflip), 1 - c)

    count = {"s": 0, "r": 0, "l": 0}
    pending = []
    save = []

    def take(kind):
        count[kind] += 1
        return count[kind] - 1

    def send(src, dst, rsem, to):
        copy = pltpu.make_async_remote_copy(
            src_ref=src, dst_ref=dst, send_sem=ss.at[take("s")], recv_sem=rsem, device_id=to, device_id_type=MESH
        )
        copy.start()
        pending.append(copy)

    def arrived(dst, rsem, frm):
        pltpu.make_async_remote_copy(
            src_ref=dst, dst_ref=dst, send_sem=ss.at[0], recv_sem=rsem, device_id=frm, device_id_type=MESH
        ).wait_recv()

    def local(src, dst):
        copy = pltpu.make_async_copy(src, dst, ls.at[take("l")])
        copy.start()
        return copy

    barrier = pltpu.get_barrier_semaphore()
    greet0 = dev(
        jnp.where(own, x, 3 - x), jnp.where(own, 3 - y, y), zh, jnp.where(own, zl, zflip), jnp.where(own, 1 - c, c)
    )
    for to in [neighbour[1], neighbour[-1], across, mirror, greet0] + list(square):
        pl.semaphore_signal(barrier, inc=1, device_id=to, device_id_type=MESH)
    pl.semaphore_wait(barrier, 8)

    def part(h):
        return pl.ds(h * PART, PART)

    s0s = [ss.at[take("s")] for _ in (0, 1)]
    s0r = [rr.at[take("r")] for _ in (0, 1)]
    s0l = [ls.at[take("l")] for _ in (0, 1)]

    def swap(src, dst_own, dst, h, start):
        @pl.when(own)
        def _():
            copy = pltpu.make_async_copy(src.at[part(h)], dst_own.at[part(h)], s0l[h])
            copy.start() if start else copy.wait()

        @pl.when(jnp.logical_not(own))
        def _():
            copy = pltpu.make_async_remote_copy(
                src_ref=src.at[part(h)], dst_ref=dst.at[part(h)], send_sem=s0s[h], recv_sem=s0r[h],
                device_id=swap0, device_id_type=MESH,
            )
            copy.start() if start else copy.wait()

    def stage0(h, start):
        swap(hid.at[0], X.at[0, held, zh], X.at[0, 1 - held, zh], h, start)

    s1r, cr, dr = rr.at[take("r")], rr.at[take("r")], rr.at[take("r")]
    stage0(0, True)
    stage0(1, True)
    send(hid.at[1], relay, s1r, mirror)
    s2s, s2r, s2l = ss.at[take("s")], rr.at[take("r")], ls.at[take("l")]

    def stage1(start):
        @pl.when(own)
        def _():
            copy = pltpu.make_async_copy(relay, X.at[1, held, zh], s2l)
            copy.start() if start else copy.wait()

        @pl.when(jnp.logical_not(own))
        def _():
            copy = pltpu.make_async_remote_copy(
                src_ref=relay, dst_ref=X.at[1, 1 - held, zh], send_sem=s2s, recv_sem=s2r,
                device_id=swap0, device_id_type=MESH,
            )
            copy.start() if start else copy.wait()

    mine = pl.ds(pl.multiple_of(qb * QUARTER, QUARTER), QUARTER)
    theirs = pl.ds(pl.multiple_of((1 - qb) * QUARTER, QUARTER), QUARTER)
    load_wq = local(wq.at[0, mine], Wq.at[xb])
    load_wkv = local(wkv.at[0, :, mine], Wkv.at[xb])
    wr = (rr.at[take("r")], rr.at[take("r")])
    send(wq.at[0, theirs], Wq.at[xb], wr[0], pair)
    send(wkv.at[0, :, theirs], Wkv.at[xb], wr[1], pair)
    load_c = local(cot.at[0], C.at[0])
    send(cot.at[1], C.at[1], cr, mirror)
    send(doc.at[1], docs, dr, mirror)
    Pq[...] = jnp.zeros_like(Pq)
    Pkv[...] = jnp.zeros_like(Pkv)

    def features(zs):
        return pl.ds(pl.multiple_of(zs * FEAT, FEAT), FEAT)

    def kv_weights(rows):
        return Wkv[:, :, rows].reshape(HEAD, FEAT)

    def project(e, d, zs):
        rows = features(zs)
        block = X[e, d, zs]
        for s in (0, 1):
            Pq[e, d, s] += dot(block, Wq[s, rows, :], 1, 0)
        Pkv[e, d] += dot(block, kv_weights(rows), 1, 1)

    def cut(h, half):
        if half is None:
            return part(h)
        return pl.ds(h * PART + half * (PART // 2), PART // 2)

    def slot(e, h, d, k, half):
        return X.at[e, d, up(zh, k), cut(h, half)], ra.at[e, h, d, up(zh, k), half or 0]

    def pass_on(e, h, k, half, sign):
        ref, sem = slot(e, h, held, k, half)
        send(ref, ref, sem, neighbour[sign])

    def got(e, h, k, half, sign):
        ref, sem = slot(e, h, held, k, half)
        arrived(ref, sem, neighbour[sign])

    def share(e, h, k):
        ref, sem = slot(e, h, held, k, None)
        send(ref, ref, sem, across)

    def shared(e, k):
        for h in (0, 1):
            ref, sem = slot(e, h, 1 - held, k, None)
            arrived(ref, sem, across)

    def gather_first(e, h):
        pass_on(e, h, 0, None, 1)
        pass_on(e, h, 0, None, -1)
        share(e, h, 0)

    def gather_second(e, h):
        got(e, h, -1, None, -1)
        pass_on(e, h, -1, 0, 1)
        share(e, h, -1)
        got(e, h, 1, None, 1)
        pass_on(e, h, 1, 1, -1)
        share(e, h, 1)

    def gather_third(e, h):
        got(e, h, 2, 0, -1)
        got(e, h, 2, 1, 1)
        share(e, h, 2)

    ORDER = (0, -1, 1, 2)

    def project_held(e):
        for k in ORDER:
            project(e, held, up(zh, k))

    def project_shared(e):
        for k in ORDER:
            shared(e, k)
            project(e, 1 - held, up(zh, k))

    cosw, sinw = cosf[...], sinf[...]

    def rope(v):
        return v * cosw + pltpu.roll(v, 64, 1) * sinw

    def unrope(v):
        return v * cosw - pltpu.roll(v, 64, 1) * sinw

    zto = {1: neighbour[1], 2: neighbour[2], 3: neighbour[-1]}
    zfrom = {1: neighbour[-1], 2: neighbour[2], 3: neighbour[1]}

    def three():
        return [[rr.at[take("r")] for _ in range(3)] for e in (0, 1)]

    prq, prk, kvr, gr, xrq, xrk = three(), three(), three(), three(), three(), three()
    ar = rr.at[take("r")]
    members = ((zl, 1 - xb), (zflip, xb), (zflip, 1 - xb))
    scale = HEAD**-0.5

    def send_partial(e):
        for d in (0, 1):
            for s in (0, 1):
                PkvP[e, d, s] = pack(Pkv[e, d, :, 64 * s : 64 * s + 64])
        for i, (d, s) in enumerate(members):
            sPkv[e, i] = PkvP[e, d, s].astype(BF16)
            send(sPkv.at[e, i], rPkv.at[e, i], prk[e][i], square[i])
        for i, (d, s) in enumerate(members):
            sPq[e, i] = Pq[e, d, s].astype(BF16)
            send(sPq.at[e, i], rPq.at[e, i], prq[e][i], square[i])

    def send_kv(e):
        piece = PkvP[e, zl, xb]
        for i in range(3):
            arrived(rPkv.at[e, i], prk[e][i], square[i])
            piece = piece + rPkv[e, i].astype(F32)
        KV[e, zh] = piece.astype(BF16)
        for o in (2, 1, 3):
            send(KV.at[e, zh], KV.at[e, zh], kvr[e][o - 1], zto[o])
        q = Pq[e, zl, xb]
        for i in range(3):
            arrived(rPq.at[e, i], prq[e][i], square[i])
            q = q + rPq[e, i].astype(F32)
        Qb[e, 0] = rope(q[:, :HEAD]).astype(BF16)
        Qb[e, 1] = rope(q[:, HEAD:]).astype(BF16)

    def attend(e):
        if e == 0:
            load_c.wait()
        else:
            arrived(C.at[1], cr, mirror)
            arrived(docs, dr, mirror)
        row = lax.broadcasted_iota(jnp.int32, (TOK, TOK), 0)
        col = lax.broadcasted_iota(jnp.int32, (TOK, TOK), 1)
        ids = doc[0] if e == 0 else docs[...]
        wide = jnp.broadcast_to(ids.astype(F32), (TOK, TOK))
        allowed = (wide == wide.T) & (col <= row)
        for o in (1, 2, 3):
            arrived(KV.at[e, up(zh, -o)], kvr[e][o - 1], zfrom[o])
        kraw = jnp.concatenate([unpack(KV[e, 0]), unpack(KV[e, 1])], axis=1)
        keys = rope(kraw).astype(BF16)
        values = jnp.concatenate([unpack(KV[e, 2]), unpack(KV[e, 3])], axis=1).astype(BF16)
        gk = jnp.zeros((TOK, HEAD), F32)
        gv = jnp.zeros((TOK, HEAD), F32)
        for j in (0, 1):
            q = Qb[e, j]
            g = C[e, :, j * HEAD : (j + 1) * HEAD]
            weights = jnp.where(allowed, jnp.exp(dot(q, keys, 1, 1) * scale), 0.0)
            probs = weights / jnp.sum(weights, axis=-1, keepdims=True)
            low = probs.astype(BF16)
            att[e, :, j * HEAD : (j + 1) * HEAD] = dot(low, values, 1, 0).astype(BF16)
            gv = gv + dot(low, g, 0, 0)
            gp = dot(g, values, 1, 1)
            rdot = jnp.sum(gp * probs, axis=-1, keepdims=True)
            gs = (probs * (gp - rdot) * scale).astype(BF16)
            Gq[e, zl, xb, :, j * HEAD : (j + 1) * HEAD] = unrope(dot(gs, keys, 1, 0)).astype(BF16)
            gk = gk + dot(gs, q, 0, 0)
        gk = unrope(gk)
        for i, v in enumerate((gk[:, :64], gk[:, 64:], gv[:, :64], gv[:, 64:])):
            v = pack(v)
            gfp[e, i] = v
            gsb[e, i] = v.astype(BF16)
        for o in (2, 1, 3):
            send(gsb.at[e, up(zh, o)], grb.at[e, o - 1], gr[e][o - 1], zto[o])
        for i in range(3):
            send(Gq.at[e, zl, xb], Gq.at[e, zl, xb], xrq[e][i], square[i])
        if e == 0:
            save.append(local(att.at[0], att_out.at[0]))
        else:
            send(att.at[1], att_out.at[1], ar, mirror)

    def send_gkv(e):
        total = gfp[e, zh]
        for o in (1, 2, 3):
            arrived(grb.at[e, o - 1], gr[e][o - 1], zfrom[o])
            total = total + grb[e, o - 1].astype(F32)
        Gkvp[e, zl, xb] = total.astype(BF16)
        for i in range(3):
            send(Gkvp.at[e, zl, xb], Gkvp.at[e, zl, xb], xrk[e][i], square[i])

    def take_g(e):
        for i, (d, s) in enumerate(members):
            arrived(Gq.at[e, d, s], xrq[e][i], square[i])
            arrived(Gkvp.at[e, d, s], xrk[e][i], square[i])
        for d in (0, 1):
            Gkv[e, d] = jnp.concatenate([unpack(Gkvp[e, d, 0]), unpack(Gkvp[e, d, 1])], axis=1).astype(BF16)

    def term(e, d, zs, h):
        rows = features(zs)
        v = dot(Gkv[e, d, part(h)], kv_weights(rows), 1, 0)
        for s in (0, 1):
            v = v + dot(Gq[e, d, s, part(h)], Wq[s, rows, :], 1, 1)
        return v

    BACK = (2, 1, -1, 0)

    def sems(n):
        return [[[rr.at[take("r")] for _ in range(n)] for h in (0, 1)] for e in (0, 1)]

    xs_r, zdr, znr = sems(4), sems(2), sems(2)

    def fars(e):
        for i, k in enumerate(BACK):
            for h in (0, 1):
                sd[e, i, part(h)] = term(e, 1 - held, up(zh, k), h).astype(BF16)
                send(sd.at[e, i, part(h)], rd.at[e, i, part(h)], xs_r[e][h][i], across)

    def add_half(v, other, half):
        n = PART // 2
        other = other.astype(F32)
        if half == 0:
            return jnp.concatenate([v[:n] + other, v[n:]], axis=0)
        return jnp.concatenate([v[:n], v[n:] + other], axis=0)

    def scatter_own(e, h, i):
        k, rows = BACK[i], part(h)
        v = term(e, held, up(zh, k), h)
        arrived(rd.at[e, i, rows], xs_r[e][h][i], across)
        v = v + rd[e, i, rows].astype(F32)
        if k == 2:
            zsd[e, rows] = v.astype(BF16)
            for half, sign in ((0, 1), (1, -1)):
                send(zsd.at[e, cut(h, half)], zrd.at[e, cut(h, half)], zdr[e][h][half], neighbour[sign])
        elif k in (1, -1):
            half, out, into = (0, zsp, zrp) if k == 1 else (1, zsm, zrm)
            arrived(zrd.at[e, cut(h, half)], zdr[e][h][half], neighbour[-k])
            v = add_half(v, zrd[e, cut(h, half)], half)
            out[e, rows] = v.astype(BF16)
            send(out.at[e, rows], into.at[e, rows], znr[e][h][half], neighbour[k])
        else:
            for half, sign, into in ((0, 1, zrp), (1, -1, zrm)):
                arrived(into.at[e, rows], znr[e][h][half], neighbour[-sign])
                v = v + into[e, rows].astype(F32)
            fin[e, rows] = v.astype(BF16)

    wsr = [(rr.at[take("r")], rr.at[take("r")]) for _ in range(4)]

    def rows_out(zs, quarter):
        start = quarter * QUARTER + zs * FEAT
        return pl.ds(pl.multiple_of(start, FEAT), FEAT)

    def query_grads(zs, s):
        t = jnp.zeros((FEAT, TOK), F32)
        for e in (0, 1):
            for d in (0, 1):
                t = t + dot(X[e, d, zs], Gq[e, d, s], 0, 0)
        return t.astype(BF16)

    def weight_grads_pair(zs):
        rows = rows_out(zs, qb)
        wgq[1, zs] = query_grads(zs, 1 - xb)
        send(wgq.at[1, zs], gq_out.at[rows], wsr[zs][0], pair)
        t = jnp.zeros((HEAD, FEAT), F32)
        for e in (0, 1):
            for d in (0, 1):
                t = t + dot(Gkv[e, d], X[e, d, zs], 0, 0)
        wgkv[zs] = t.astype(BF16).reshape(2, 64, FEAT)
        send(wgkv.at[zs, 1 - xb], gkv_out.at[:, rows], wsr[zs][1], pair)
        save.append(local(wgkv.at[zs, xb], gkv_out.at[:, rows]))

    def weight_grads_own(zs):
        wgq[0, zs] = query_grads(zs, xb)
        save.append(local(wgq.at[0, zs], gq_out.at[rows_out(zs, qb)]))

    f1r = [rr.at[take("r")] for _ in (0, 1)]

    def final0(h, start):
        swap(fin.at[0], hg_out.at[0], hg_out.at[0], h, start)

    for h in (0, 1):
        stage0(h, False)
        gather_first(0, h)
    arrived(relay, s1r, mirror)
    stage1(True)
    gather_second(0, 0)
    gather_second(0, 1)
    stage1(False)
    gather_first(1, 0)
    gather_first(1, 1)
    gather_third(0, 0)
    gather_third(0, 1)
    load_wq.wait()
    load_wkv.wait()
    arrived(Wq.at[1 - xb], wr[0], pair)
    arrived(Wkv.at[1 - xb], wr[1], pair)
    project_held(0)
    gather_second(1, 0)
    gather_second(1, 1)
    for k in ORDER:
        shared(0, k)
        project(0, 1 - held, up(zh, k))
    send_partial(0)
    gather_third(1, 0)
    gather_third(1, 1)
    send_kv(0)
    attend(0)
    project_held(1)
    send_gkv(0)
    project_shared(1)
    send_partial(1)
    take_g(0)
    fars(0)
    send_kv(1)
    scatter_own(0, 0, 0)
    scatter_own(0, 1, 0)
    attend(1)
    scatter_own(0, 0, 1)
    scatter_own(0, 1, 1)
    send_gkv(1)
    scatter_own(0, 0, 2)
    scatter_own(0, 1, 2)
    take_g(1)
    fars(1)
    for h in (0, 1):
        scatter_own(0, h, 3)
        final0(h, True)
    weight_grads_pair(0)
    weight_grads_pair(1)
    scatter_own(1, 0, 0)
    scatter_own(1, 1, 0)
    weight_grads_pair(2)
    weight_grads_pair(3)
    for i in (1, 2):
        for h in (0, 1):
            scatter_own(1, h, i)
    weight_grads_own(0)
    weight_grads_own(1)
    for h in (0, 1):
        scatter_own(1, h, 3)
        send(fin.at[1, part(h)], hg_out.at[1, part(h)], f1r[h], swap1)
    weight_grads_own(2)
    weight_grads_own(3)
    for h in (0, 1):
        final0(h, False)
        arrived(hg_out.at[1, part(h)], f1r[h], swap1)
    arrived(att_out.at[1], ar, mirror)
    for zs in range(4):
        rows = rows_out(zs, 1 - qb)
        arrived(gq_out.at[rows], wsr[zs][0], pair)
        arrived(gkv_out.at[:, rows], wsr[zs][1], pair)
    for copy in save:
        copy.wait()
    for copy in pending:
        copy.wait_send()


def finish(att, hg, gq, gkv, att_out, hg_out, gq_out, gkv_out):
    att_out[...] = att[...]
    hg_out[...] = hg[...]
    gq_out[...] = gq[...].astype(F32)
    gkv_out[...] = gkv[...].astype(F32)


def rope_tables():
    freqs = 10000.0 ** (-2.0 * np.arange(HEAD // 2) / HEAD)
    angles = np.arange(TOK, dtype=np.float32)[:, None] * freqs.astype(np.float32)[None, :]
    cosine, sine = np.cos(angles), np.sin(angles)
    return (
        np.concatenate([cosine, cosine], 1).astype(np.float32),
        np.concatenate([-sine, sine], 1).astype(np.float32),
    )


def body(hidden, query_weight, keyval_weight, doc_ids, cotangent):
    cosf, sinf = rope_tables()
    anywhere = pl.BlockSpec(memory_space=pl.ANY)
    vmem = pl.BlockSpec(memory_space=pltpu.VMEM)
    V = pltpu.VMEM
    big = V((2, 4, TOK, FEAT), BF16)
    mid = V((2, TOK, FEAT), BF16)
    scratch = [
        V((2, 2, 4, TOK, FEAT), BF16), V((TOK, FEAT), BF16),
        V((2, QUARTER, 256), BF16), V((2, 64, QUARTER), BF16),
        V((2, TOK, 256), BF16), V((1, TOK), jnp.int32),
        V((2, 2, 2, TOK, 256), F32), V((2, 2, TOK, 128), F32), V((2, 2, 2, 128, 128), F32),
        V((2, 3, TOK, 256), BF16), V((2, 3, 128, 128), BF16), V((2, 3, TOK, 256), BF16), V((2, 3, 128, 128), BF16),
        V((2, 4, 128, 128), BF16),
        V((2, 4, 128, 128), F32), V((2, 4, 128, 128), BF16), V((2, 3, 128, 128), BF16),
        V((2, 2, 2, TOK, 256), BF16), V((2, 2, 2, 128, 128), BF16), V((2, 2, TOK, 128), BF16),
        V((2, 2, TOK, HEAD), BF16),
        V((2, TOK, 256), BF16),
        big, big,
        mid, mid, mid, mid, mid, mid, mid,
        V((2, 4, FEAT, 256), BF16), V((4, 2, 64, FEAT), BF16),
        pltpu.SemaphoreType.DMA((160,)),
        pltpu.SemaphoreType.DMA((128,)),
        pltpu.SemaphoreType.DMA((2, 2, 2, 4, 2)),
        pltpu.SemaphoreType.DMA((32,)),
    ]
    att, hg, gq, gkv = pl.pallas_call(
        kernel,
        out_shape=(
            jax.ShapeDtypeStruct((2, TOK, 256), BF16),
            jax.ShapeDtypeStruct((2, TOK, FEAT), BF16),
            jax.ShapeDtypeStruct((4096, 256), BF16),
            jax.ShapeDtypeStruct((64, 4096), BF16),
        ),
        in_specs=[anywhere, anywhere, anywhere, vmem, anywhere, vmem, vmem],
        out_specs=(anywhere,) * 4,
        scratch_shapes=scratch,
        compiler_params=pltpu.CompilerParams(
            collective_id=0, has_side_effects=True, vmem_limit_bytes=60 * 2**20
        ),
    )(hidden[0], query_weight[0], keyval_weight[0].swapaxes(1, 2), doc_ids[0], cotangent[0], cosf, sinf)
    steps = 4
    specs = (
        pl.BlockSpec((2, TOK // steps, 256), lambda i: (0, i, 0)),
        pl.BlockSpec((2, TOK // steps, FEAT), lambda i: (0, i, 0)),
        pl.BlockSpec((4096 // steps, 256), lambda i: (i, 0)),
        pl.BlockSpec((64, 4096 // steps), lambda i: (0, i)),
    )
    att, hg, gq, gkv = pl.pallas_call(
        finish,
        grid=(steps,),
        out_shape=(
            jax.ShapeDtypeStruct(att.shape, BF16),
            jax.ShapeDtypeStruct(hg.shape, BF16),
            jax.ShapeDtypeStruct(gq.shape, F32),
            jax.ShapeDtypeStruct(gkv.shape, F32),
        ),
        in_specs=list(specs),
        out_specs=specs,
        compiler_params=pltpu.CompilerParams(vmem_limit_bytes=60 * 2**20),
    )(att, hg, gq, gkv)
    return att[None], hg[None], gq[None], gkv.T[None]


def solution(mesh):
    sharded = P("pipe", None, "dp", "tensor")
    return jax.shard_map(
        body,
        mesh=mesh,
        in_specs=(sharded, sharded, sharded, P("pipe", None, "dp", None), sharded),
        out_specs=(sharded, sharded, P("pipe", "dp", "tensor"), P("pipe", "dp", "tensor")),
        check_vma=False,
    )
```
